32 devices in a mesh: dp: 2 (over x), fsdp: 4 (over y, core), tensor: 4 (over z).
Axes of the slice: x: 2, y: 2, z: 4, core: 2. Of those that a mesh axis runs over, the one named last changes fastest.
Arguments:
- tokens: bfloat16 [4096, 576], P(('dp', 'fsdp', 'tensor')), may hold values from -6 to 6
- gate_weight: bfloat16 [576, 1536], P('fsdp', 'tensor'), may hold values from -0.25 to 0.25
- up_weight: bfloat16 [576, 1536], P('fsdp', 'tensor'), may hold values from -0.25 to 0.25
- down_weight: bfloat16 [1536, 576], P('tensor', 'fsdp'), may hold values from -0.15625 to 0.15625
- cotangent: bfloat16 [4096, 576], P(('dp', 'fsdp', 'tensor')), may hold values from -0.119628906 to 0.119628906
Outputs:
- mixed: bfloat16 [4096, 576], P(('dp', 'fsdp', 'tensor'))
- grad_tokens: bfloat16 [4096, 576], P(('dp', 'fsdp', 'tensor'))
- grad_gate_weight: bfloat16 [576, 1536], P('fsdp', 'tensor')
- grad_up_weight: bfloat16 [576, 1536], P('fsdp', 'tensor')
- grad_down_weight: bfloat16 [1536, 576], P('tensor', 'fsdp')
The draws below stay inside these ranges and needn't reach their ends.
All inputs are finite; a program needn't handle non-finite values.
Results may differ from the reference program's by a relative error of at most 0.025.
Values may be sent and summed in bfloat16 or wider, within the bound.
No kernel may reach another device: no remote copies, remote signals or barrier semaphores. Data moves between devices by JAX's collectives and lax.ppermute only.
A program may use at most 64 MiB of HBM per device.

```python
import math
import jax
import jax.numpy as jnp
from jax import lax

D = 576
FF = 1536
TOKENS = 4096
N_TENSOR = 4


def block_levels(stream_key, shape, split, smallest, high):
    gain = 1.0
    for dim, blocks in split:
        heights = jax.random.uniform(jax.random.fold_in(jax.random.fold_in(stream_key, 6), dim), (blocks,), jnp.float32, smallest / len(split), high / len(split))
        gain = gain * jnp.repeat(jnp.exp(heights), shape[dim] // blocks).reshape((-1,) + (1,) * (len(shape) - 1 - dim))
    return gain


def centred(key, extent, scale, most, cuts=(), kind=jnp.bfloat16):
    loudness = block_levels(key, extent, cuts, -0.22, 0.18) if cuts else 1.0
    array = jax.random.normal(key, extent, jnp.float32) * scale * loudness
    return jnp.minimum(jnp.maximum(array, -most), most).astype(kind)


def setup_inputs(seed: int = 0) -> dict:
    seeds = jax.random.split(jax.random.key(seed), 6)
    return {
        "tokens": centred(seeds[0], (TOKENS, D), 1.0, 6.0, ((0, 32),)),
        "gate_weight": centred(seeds[1], (D, FF), D ** -0.5, 0.25, ((0, 4), (1, 4))),
        "up_weight": centred(seeds[2], (D, FF), D ** -0.5, 0.25, ((0, 4), (1, 4))),
        "down_weight": centred(seeds[3], (FF, D), FF ** -0.5, 0.15625, ((0, 4), (1, 4))),
        "cotangent": centred(seeds[4], (TOKENS, D), 0.02, 0.119628906, ((0, 32),)),
    }


def activate(gate_sum, up_sum):
    sig = jax.nn.sigmoid(gate_sum)
    swished = gate_sum * sig
    slopes = up_sum * sig * (1.0 + gate_sum * (1.0 - sig))
    hidden = (swished * up_sum).astype(jnp.bfloat16)
    return hidden, swished, slopes


def inner_rows(left, right):
    return lax.dot_general(left, right, (((0,), (0,)), ((), ())), preferred_element_type=jnp.float32)


def inner_cols(left, right):
    return lax.dot_general(left, right, (((1,), (1,)), ((), ())), preferred_element_type=jnp.float32)


def group_sum(pairs, blocks):
    total = None
    for left, right in pairs:
        rows = left.shape[0]
        width = left.shape[1] // blocks
        left_blocks = left.reshape(rows, blocks, width).astype(jnp.float32)
        right_blocks = right.reshape(blocks, width, right.shape[1]).astype(jnp.float32)
        term = jnp.einsum("rtk,tkd->trd", left_blocks, right_blocks)
        total = term if total is None else total + term
    rounded = lax.optimization_barrier(total.astype(jnp.bfloat16))
    return jnp.sum(rounded.astype(jnp.float32), axis=0)


def reference(tokens, gate_weight, up_weight, down_weight, cotangent):
    block = math.gcd(TOKENS, 4096)
    count = TOKENS // block
    gate_back = gate_weight.T
    up_back = up_weight.T

    def step(carry, index):
        acc_gate, acc_up, acc_down = carry
        first = (index * block).astype(jnp.int32)
        rows = lax.dynamic_slice_in_dim(tokens, first, block, 0)
        cot_rows = lax.dynamic_slice_in_dim(cotangent, first, block, 0)
        gate_sum = jnp.dot(rows, gate_weight, preferred_element_type=jnp.float32)
        up_sum = jnp.dot(rows, up_weight, preferred_element_type=jnp.float32)
        hidden, swished, slopes = activate(gate_sum, up_sum)
        mixed = group_sum(((hidden, down_weight),), N_TENSOR).astype(jnp.bfloat16)
        grad_hidden = inner_cols(cot_rows, down_weight)
        grad_gate = (grad_hidden * slopes).astype(jnp.bfloat16)
        grad_up = (grad_hidden * swished).astype(jnp.bfloat16)
        grad_rows = group_sum(((grad_gate, gate_back), (grad_up, up_back)), N_TENSOR).astype(jnp.bfloat16)
        acc_gate = acc_gate + inner_rows(rows, grad_gate)
        acc_up = acc_up + inner_rows(rows, grad_up)
        acc_down = acc_down + inner_rows(hidden, cot_rows)
        return (acc_gate, acc_up, acc_down), (mixed, grad_rows)

    start = (jnp.zeros((D, FF), jnp.float32), jnp.zeros((D, FF), jnp.float32), jnp.zeros((FF, D), jnp.float32))
    sums, outs = lax.scan(step, start, jnp.arange(count, dtype=jnp.int32))
    mixed = outs[0].reshape(TOKENS, D)
    grad_tokens = outs[1].reshape(TOKENS, D)
    return mixed, grad_tokens, sums[0].astype(jnp.bfloat16), sums[1].astype(jnp.bfloat16), sums[2].astype(jnp.bfloat16)
```

```python
import functools

import jax
import jax.numpy as jnp
from jax import lax
from jax.experimental import pallas as pl
from jax.experimental.pallas import tpu as pltpu
from jax.sharding import PartitionSpec as P

BF16, F32 = jnp.bfloat16, jnp.float32
SCOPED_BYTES = 16 * 1024 * 1024


def contract(left, right, left_dim, right_dim):
    return lax.dot_general(left, right, (((left_dim,), (right_dim,)), ((), ())), preferred_element_type=F32)


def exchange(array, axis, mask):
    return lax.ppermute(array, axis, [(i, i ^ mask) for i in range(lax.axis_size(axis))])


def call(body, outs, operands, inside=pltpu.VMEM, outside=False, scratch=()):
    whole = pl.BlockSpec(memory_space=pltpu.VMEM)
    kind = jax.ShapeDtypeStruct if outside else pltpu.VMEM
    return pl.pallas_call(
        body,
        out_shape=[kind(shape, dtype) for shape, dtype in outs],
        in_specs=[pl.BlockSpec(memory_space=inside)] * len(operands),
        out_specs=[whole] * len(outs),
        scratch_shapes=list(scratch),
        cost_estimate=pl.CostEstimate(flops=1, bytes_accessed=1, transcendentals=0),
        compiler_params=pltpu.CompilerParams(vmem_limit_bytes=SCOPED_BYTES),
    )(*[pltpu.with_memory_space_constraint(operand, inside) for operand in operands])


def stack_kernel(counts, *refs):
    arrays, stacks, sems = refs[: sum(counts)], refs[sum(counts):-1], refs[-1]
    places = [stack.at[i] for stack, count in zip(stacks, counts) for i in range(count)]
    copies = [pltpu.make_async_copy(array, place, sems.at[i]) for i, (array, place) in enumerate(zip(arrays, places))]
    for copy in copies:
        copy.start()
    for copy in copies:
        copy.wait()


def stack(*groups):
    arrays = [array for group in groups for array in group]
    return call(
        functools.partial(stack_kernel, [len(group) for group in groups]),
        [((len(group), *group[0].shape), group[0].dtype) for group in groups],
        arrays,
        inside=pltpu.HBM,
        scratch=[pltpu.SemaphoreType.DMA((len(arrays),))],
    )


def join_kernel(*refs):
    runs, joined = refs[:-1], refs[-1]
    first = 0
    for run in runs:
        joined[first:first + run.shape[0]] = run[...]
        first += run.shape[0]


def assemble_kernel(masks, *refs):
    blocks, (whole, turned) = refs[: len(masks)], refs[len(masks):]
    index = lax.axis_index("fsdp")
    rows = blocks[0].shape[1]
    for mask, block in zip(masks, blocks):
        start = pl.multiple_of((index ^ mask) * rows, 16)
        whole[:, pl.ds(start, rows), :] = block[...]
    for i in range(whole.shape[0]):
        turned[i] = whole[i].T


def forward(turned, rows):
    gate_sum = contract(turned[0], rows, 1, 0)
    up_sum = contract(turned[1], rows, 1, 0)
    sig = 1.0 / (1.0 + jnp.exp(-gate_sum))
    swished = gate_sum * sig
    slopes = up_sum * sig * (1.0 + gate_sum * (1.0 - sig))
    return (swished * up_sum).astype(BF16), swished, slopes


def block_grads(turned, blocks):
    rows = jnp.concatenate([block[0] for block in blocks], axis=1)
    columns = jnp.concatenate([block[1] for block in blocks], axis=1)
    hidden, swished, slopes = forward(turned, rows)
    grad_hidden = contract(turned[2], columns, 1, 0)
    grad_gate = (grad_hidden * slopes).astype(BF16)
    grad_up = (grad_hidden * swished).astype(BF16)
    return rows, columns, hidden, grad_gate, grad_up


def token_parts(whole, hidden, grad_gate, grad_up, parts):
    out = contract(whole[2], hidden, 1, 0)
    back = contract(whole[0], grad_gate, 1, 0) + contract(whole[1], grad_up, 1, 0)
    width = out.shape[1] // len(parts)
    rows = out.shape[0]
    for i, part in enumerate(parts):
        part[0, :rows] = out[:, i * width:(i + 1) * width].astype(part.dtype)
        part[1, :rows] = back[:, i * width:(i + 1) * width].astype(part.dtype)
        if part.shape[1] > rows:
            part[:, rows:] = jnp.zeros((2, part.shape[1] - rows, width), part.dtype)


def weight_terms(rows, columns, hidden, grad_gate, grad_up):
    return ((rows, grad_gate), (rows, grad_up), (columns, hidden))


def group_kernel(count, first, whole, turned, *refs):
    blocks, refs = refs[:count], refs[count:]
    before, (after, *parts) = (None, refs) if first else (refs[0], refs[1:])
    rows, columns, hidden, grad_gate, grad_up = block_grads(turned, blocks)
    for i, (left, right) in enumerate(weight_terms(rows, columns, hidden, grad_gate, grad_up)):
        term = contract(left, right, 1, 1)
        after[i] = term if first else before[i] + term
    token_parts(whole, hidden, grad_gate, grad_up, parts)


def last_kernel(whole, turned, block, _, hidden_out, gate_out, up_out, part):
    _, _, hidden, grad_gate, grad_up = block_grads(turned, [block])
    hidden_out[...], gate_out[...], up_out[...] = hidden, grad_gate, grad_up
    token_parts(whole, hidden, grad_gate, grad_up, [part])


def share_kernel(other, block, hidden, grad_gate, grad_up, before, *outs):
    own = lax.axis_index("fsdp") % 2
    pick = 1 - own if other else own
    pairs, size = outs[0].shape[:2]
    for i, (side, right) in enumerate(((0, grad_gate), (0, grad_up), (1, hidden))):
        for pair in range(pairs):
            start = pl.multiple_of((2 * pair + pick) * size, 16)
            term = contract(block[side, pl.ds(start, size), :], right[...], 1, 1)
            outs[i][pair] = (before[i, pl.ds(start, size), :] + term).astype(outs[i].dtype)


def pair_sums(count, refs):
    kept, received = refs[:count], refs[count:2 * count]
    return lambda i, pair: (kept[i][pair] + received[i][pair].astype(F32)).astype(BF16)


def whole_parts_kernel(count, *refs):
    sums, parts = pair_sums(count, refs), refs[2 * count:]
    index = lax.axis_index("fsdp") // 2
    for mask, part in enumerate(parts):
        for i in range(count):
            part[i] = sums(i, index ^ mask)


def split_parts_kernel(count, *refs):
    sums, parts, rows = pair_sums(count, refs), refs[2 * count:-1], refs[-1]
    index, own = lax.axis_index("fsdp") // 2, lax.axis_index("dp")
    size, length = rows.shape[0] // count, parts[0].shape[0]
    for mask in range(len(parts) // 2):
        for i in range(count):
            rows[i * size:(i + 1) * size] = sums(i, index ^ mask)
        for flip in range(2):
            start = pl.multiple_of((own ^ flip) * (rows.shape[0] - length), 16)
            parts[2 * mask + flip][...] = rows[pl.ds(start, length), :]


def add_kernel(*refs):
    total = refs[0][...].astype(F32)
    for ref in refs[1:-1]:
        total = total + ref[...].astype(F32)
    refs[-1][...] = total.astype(BF16)


def merge_kernel(count, mine, other, *refs):
    outs, rows = refs[:count], refs[count]
    first = lax.axis_index("dp") == 0
    length = mine.shape[0]
    rows[:length] = jnp.where(first, mine[...], other[...])
    rows[rows.shape[0] - length:] = jnp.where(first, other[...], mine[...])
    size = rows.shape[0] // count
    for i, out in enumerate(outs):
        out[...] = rows[i * size:(i + 1) * size]


def middle_kernel(part, received, *refs):
    total = refs[-1]
    total[...] = (part[...] + received[...].astype(F32)).astype(BF16)


def rows_sum_kernel(count, own, *refs):
    received, outs = refs[:count], refs[count:]
    for i, out in enumerate(outs):
        total = own[i]
        for ref in received:
            total = total + ref[i, :out.shape[0]].astype(F32)
        out[...] = total.astype(BF16)


def per_device(tokens, gate_weight, up_weight, down_weight, cotangent):
    tensor, fsdp, dp = (lax.axis_size(axis) for axis in ("tensor", "fsdp", "dp"))
    own_count, width = tokens.shape
    rows, hidden_width = gate_weight.shape

    block, weight = {}, {}
    own_weights = [gate_weight, up_weight, down_weight.T]
    block[0], = stack([tokens.T, cotangent.T])
    weight[0], *runs = stack(own_weights, own_weights[:2], own_weights[2:])
    even, odd = list(range(2, tensor, 2)), list(range(3, tensor, 2))
    for mask in even + [1]:
        block[mask] = exchange(block[0], "tensor", mask)
    for mask in odd:
        block[mask - 1], block[1] = lax.optimization_barrier((block[mask - 1], block[1]))
        block[mask] = exchange(block[mask - 1], "tensor", 1)
    masks = list(range(fsdp))
    weight[1] = exchange(weight[0], "fsdp", 1)
    for mask in masks[2::2]:
        weight[mask], = call(
            join_kernel, [(weight[0].shape, BF16)], [exchange(run, "fsdp", mask) for run in runs]
        )
        weight[mask + 1] = exchange(weight[mask], "fsdp", 1)
    whole, turned = call(
        functools.partial(assemble_kernel, masks),
        [((3, width, hidden_width), BF16), ((3, hidden_width, width), BF16)],
        [weight[mask] for mask in masks],
    )

    part_shape = (2, width, own_count)
    sums_shape = ((3, width, hidden_width), F32)
    sums, part = [], {}
    for group in [[0, 1]] + [[mask] for mask in even + odd[:-1]]:
        kinds = {mask: (part_shape, BF16 if mask % 2 else F32) for mask in group}
        if 1 in group:
            kinds[1] = ((2, width + 16, own_count), BF16)
        sums, *parts = call(
            functools.partial(group_kernel, len(group), 0 in group),
            [sums_shape] + [kinds[mask] for mask in group],
            [whole, turned] + [block[mask] for mask in group] + ([] if 0 in group else [sums]),
        )
        part.update(zip(group, parts))
    last = odd[-1]
    *state, part[last] = call(
        last_kernel,
        [((hidden_width, own_count), BF16)] * 3 + [(part_shape, BF16)],
        [whole, turned, block[last], sums],
    )
    half_shape = (fsdp // 2, rows, hidden_width)
    sent = call(functools.partial(share_kernel, True), [(half_shape, BF16)] * 3, [block[last], *state, sums])
    kept = call(functools.partial(share_kernel, False), [(half_shape, F32)] * 3, [block[last], *state, sums])

    received = [exchange(array, "fsdp", 1) for array in sent]
    if dp == 2:
        total = 3 * rows
        length = (total // 2 + 15) // 16 * 16
        half = ((length, hidden_width), BF16)
        shares = call(
            functools.partial(split_parts_kernel, 3),
            [half] * fsdp,
            [*kept, *received],
            scratch=[pltpu.VMEM((total, hidden_width), BF16)],
        )
        ready = shares[0]
        landed = [ready]
        for i, share in list(enumerate(shares))[1:]:
            mask, flip = 2 * (i // 2), i % 2
            perm = [(d * fsdp + f, (d ^ flip) * fsdp + (f ^ mask)) for d in range(dp) for f in range(fsdp)]
            landed.append(lax.ppermute(share, ("dp", "fsdp"), perm))
        mine, = call(add_kernel, [half], landed)
        grads = call(
            functools.partial(merge_kernel, 3),
            [((rows, hidden_width), BF16)] * 3,
            [mine, exchange(mine, "dp", 1)],
            outside=True,
            scratch=[pltpu.VMEM((total, hidden_width), BF16)],
        )
    else:
        blocks = call(
            functools.partial(whole_parts_kernel, 3),
            [((3, rows, hidden_width), BF16)] * (fsdp // 2),
            [*kept, *received],
        )
        ready = blocks[0]
        landed = [exchange(blocks[mask], "fsdp", 2 * mask) for mask in range(1, fsdp // 2)]
        mine, = call(add_kernel, [(ready.shape, BF16)], [ready, *landed])
        grads = lax.psum(mine, "dp")

    back = [exchange(part[1], "tensor", 1)]
    for mask in even:
        arrived = exchange(part[mask + 1], "tensor", 1)
        total, = call(middle_kernel, [(part_shape, BF16)], [part[mask], arrived, ready])
        back.append(exchange(total, "tensor", mask))
    part[0], grads = lax.optimization_barrier((part[0], grads))
    mixed, grad_tokens = call(
        functools.partial(rows_sum_kernel, len(back)),
        [((width, own_count), BF16)] * 2,
        [part[0], *back],
        outside=True,
    )
    return mixed.T, grad_tokens.T, grads[0], grads[1], grads[2].T


def solution(mesh):
    token_spec = P(("dp", "fsdp", "tensor"), None)
    return jax.shard_map(
        per_device,
        mesh=mesh,
        in_specs=(token_spec, P("fsdp", "tensor"), P("fsdp", "tensor"), P("tensor", "fsdp"), token_spec),
        out_specs=(token_spec, token_spec, P("fsdp", "tensor"), P("fsdp", "tensor"), P("tensor", "fsdp")),
        check_vma=False,
    )
```

```python
import functools

import jax
import jax.numpy as jnp
from jax import lax
from jax.experimental import pallas as pl
from jax.experimental.pallas import tpu as pltpu
from jax.sharding import PartitionSpec as P

BF16, F32 = jnp.bfloat16, jnp.float32
SCOPED_BYTES = 16 * 1024 * 1024


def contract(left, right, left_dim, right_dim):
    return lax.dot_general(left, right, (((left_dim,), (right_dim,)), ((), ())), preferred_element_type=F32)


def exchange(array, axis, mask):
    return lax.ppermute(array, axis, [(i, i ^ mask) for i in range(lax.axis_size(axis))])


def call(body, outs, operands, inside=pltpu.VMEM, outside=False, scratch=()):
    whole = pl.BlockSpec(memory_space=pltpu.VMEM)
    kind = jax.ShapeDtypeStruct if outside else pltpu.VMEM
    return pl.pallas_call(
        body,
        out_shape=[kind(shape, dtype) for shape, dtype in outs],
        in_specs=[pl.BlockSpec(memory_space=inside)] * len(operands),
        out_specs=[whole] * len(outs),
        scratch_shapes=list(scratch),
        cost_estimate=pl.CostEstimate(flops=1, bytes_accessed=1, transcendentals=0),
        compiler_params=pltpu.CompilerParams(vmem_limit_bytes=SCOPED_BYTES),
    )(*[pltpu.with_memory_space_constraint(operand, inside) for operand in operands])


def stack_kernel(counts, *refs):
    arrays, stacks, sems = refs[: sum(counts)], refs[sum(counts):-1], refs[-1]
    places = [stack.at[i] for stack, count in zip(stacks, counts) for i in range(count)]
    copies = [pltpu.make_async_copy(array, place, sems.at[i]) for i, (array, place) in enumerate(zip(arrays, places))]
    for copy in copies:
        copy.start()
    for copy in copies:
        copy.wait()


def stack(*groups):
    arrays = [array for group in groups for array in group]
    return call(
        functools.partial(stack_kernel, [len(group) for group in groups]),
        [((len(group), *group[0].shape), group[0].dtype) for group in groups],
        arrays,
        inside=pltpu.HBM,
        scratch=[pltpu.SemaphoreType.DMA((len(arrays),))],
    )


def join_kernel(*refs):
    runs, joined = refs[:-1], refs[-1]
    first = 0
    for run in runs:
        joined[first:first + run.shape[0]] = run[...]
        first += run.shape[0]


def assemble_kernel(masks, *refs):
    blocks, (whole, turned) = refs[: len(masks)], refs[len(masks):]
    index = lax.axis_index("fsdp")
    rows = blocks[0].shape[1]
    for mask, block in zip(masks, blocks):
        start = pl.multiple_of((index ^ mask) * rows, 16)
        whole[:, pl.ds(start, rows), :] = block[...]
    for i in range(whole.shape[0]):
        turned[i] = whole[i].T


def forward(turned, rows):
    gate_sum = contract(turned[0], rows, 1, 0)
    up_sum = contract(turned[1], rows, 1, 0)
    sig = 1.0 / (1.0 + jnp.exp(-gate_sum))
    swished = gate_sum * sig
    slopes = up_sum * sig * (1.0 + gate_sum * (1.0 - sig))
    return (swished * up_sum).astype(BF16), swished, slopes


def block_grads(turned, blocks):
    rows = jnp.concatenate([block[0] for block in blocks], axis=1)
    columns = jnp.concatenate([block[1] for block in blocks], axis=1)
    hidden, swished, slopes = forward(turned, rows)
    grad_hidden = contract(turned[2], columns, 1, 0)
    grad_gate = (grad_hidden * slopes).astype(BF16)
    grad_up = (grad_hidden * swished).astype(BF16)
    return rows, columns, hidden, grad_gate, grad_up


def token_parts(whole, hidden, grad_gate, grad_up, parts):
    out = contract(whole[2], hidden, 1, 0)
    back = contract(whole[0], grad_gate, 1, 0) + contract(whole[1], grad_up, 1, 0)
    width = out.shape[1] // len(parts)
    rows = out.shape[0]
    for i, part in enumerate(parts):
        part[0, :rows] = out[:, i * width:(i + 1) * width].astype(part.dtype)
        part[1, :rows] = back[:, i * width:(i + 1) * width].astype(part.dtype)
        if part.shape[1] > rows:
            part[:, rows:] = jnp.zeros((2, part.shape[1] - rows, width), part.dtype)


def weight_terms(rows, columns, hidden, grad_gate, grad_up):
    return ((rows, grad_gate), (rows, grad_up), (columns, hidden))


def group_kernel(count, first, whole, turned, *refs):
    blocks, refs = refs[:count], refs[count:]
    before, (after, *parts) = (None, refs) if first else (refs[0], refs[1:])
    rows, columns, hidden, grad_gate, grad_up = block_grads(turned, blocks)
    for i, (left, right) in enumerate(weight_terms(rows, columns, hidden, grad_gate, grad_up)):
        term = contract(left, right, 1, 1)
        after[i] = term if first else before[i] + term
    token_parts(whole, hidden, grad_gate, grad_up, parts)


def last_kernel(whole, turned, block, _, hidden_out, gate_out, up_out, part):
    _, _, hidden, grad_gate, grad_up = block_grads(turned, [block])
    hidden_out[...], gate_out[...], up_out[...] = hidden, grad_gate, grad_up
    token_parts(whole, hidden, grad_gate, grad_up, [part])


def share_kernel(other, block, hidden, grad_gate, grad_up, before, *outs):
    own = lax.axis_index("fsdp") % 2
    pick = 1 - own if other else own
    pairs, size = outs[0].shape[:2]
    for i, (side, right) in enumerate(((0, grad_gate), (0, grad_up), (1, hidden))):
        for pair in range(pairs):
            start = pl.multiple_of((2 * pair + pick) * size, 16)
            term = contract(block[side, pl.ds(start, size), :], right[...], 1, 1)
            outs[i][pair] = (before[i, pl.ds(start, size), :] + term).astype(outs[i].dtype)


def pair_sums(count, refs):
    kept, received = refs[:count], refs[count:2 * count]
    return lambda i, pair: (kept[i][pair] + received[i][pair].astype(F32)).astype(BF16)


def whole_parts_kernel(count, *refs):
    sums, parts = pair_sums(count, refs), refs[2 * count:]
    index = lax.axis_index("fsdp") // 2
    for mask, part in enumerate(parts):
        for i in range(count):
            part[i] = sums(i, index ^ mask)


def split_parts_kernel(count, *refs):
    sums, parts, rows = pair_sums(count, refs), refs[2 * count:-1], refs[-1]
    index, own = lax.axis_index("fsdp") // 2, lax.axis_index("dp")
    size, length = rows.shape[0] // count, parts[0].shape[0]
    for mask in range(len(parts) // 2):
        for i in range(count):
            rows[i * size:(i + 1) * size] = sums(i, index ^ mask)
        for flip in range(2):
            start = pl.multiple_of((own ^ flip) * (rows.shape[0] - length), 16)
            parts[2 * mask + flip][...] = rows[pl.ds(start, length), :]


def add_kernel(*refs):
    total = refs[0][...].astype(F32)
    for ref in refs[1:-1]:
        total = total + ref[...].astype(F32)
    refs[-1][...] = total.astype(BF16)


def merge_kernel(count, mine, other, *refs):
    outs, rows = refs[:count], refs[count]
    first = lax.axis_index("dp") == 0
    length = mine.shape[0]
    rows[:length] = jnp.where(first, mine[...], other[...])
    rows[rows.shape[0] - length:] = jnp.where(first, other[...], mine[...])
    size = rows.shape[0] // count
    for i, out in enumerate(outs):
        out[...] = rows[i * size:(i + 1) * size]


def middle_kernel(part, received, *refs):
    total = refs[-1]
    total[...] = (part[...] + received[...].astype(F32)).astype(BF16)


def rows_sum_kernel(count, own, *refs):
    received, outs = refs[:count], refs[count:]
    for i, out in enumerate(outs):
        total = own[i]
        for ref in received:
            total = total + ref[i, :out.shape[0]].astype(F32)
        out[...] = total.astype(BF16)


def per_device(tokens, gate_weight, up_weight, down_weight, cotangent):
    tensor, fsdp, dp = (lax.axis_size(axis) for axis in ("tensor", "fsdp", "dp"))
    own_count, width = tokens.shape
    rows, hidden_width = gate_weight.shape

    block, weight = {}, {}
    own_weights = [gate_weight, up_weight, down_weight.T]
    block[0], = stack([tokens.T, cotangent.T])
    weight[0], *runs = stack(own_weights, own_weights[:2], own_weights[2:])
    straight = list(range(3, tensor, 2))
    for mask in straight + [1]:
        block[mask] = exchange(block[0], "tensor", mask)
    for mask in straight:
        block[mask], block[1] = lax.optimization_barrier((block[mask], block[1]))
        block[mask ^ 1] = exchange(block[mask], "tensor", 1)
    masks = list(range(fsdp))
    weight[1] = exchange(weight[0], "fsdp", 1)
    for mask in masks[2::2]:
        weight[mask], = call(
            join_kernel, [(weight[0].shape, BF16)], [exchange(run, "fsdp", mask) for run in runs]
        )
        weight[mask + 1] = exchange(weight[mask], "fsdp", 1)
    whole, turned = call(
        functools.partial(assemble_kernel, masks),
        [((3, width, hidden_width), BF16), ((3, hidden_width, width), BF16)],
        [weight[mask] for mask in masks],
    )

    part_shape = (2, width, own_count)
    sums_shape = ((3, width, hidden_width), F32)
    sums, part = [], {}
    forwarded = [mask ^ 1 for mask in straight]
    last = forwarded[-1]
    for group in [[0, 1]] + [[mask] for mask in straight + forwarded[:-1]]:
        kinds = {mask: (part_shape, BF16 if mask in forwarded else F32) for mask in group}
        if 1 in group:
            kinds[1] = ((2, width + 16, own_count), BF16)
        sums, *parts = call(
            functools.partial(group_kernel, len(group), 0 in group),
            [sums_shape] + [kinds[mask] for mask in group],
            [whole, turned] + [block[mask] for mask in group] + ([] if 0 in group else [sums]),
        )
        part.update(zip(group, parts))
    *state, part[last] = call(
        last_kernel,
        [((hidden_width, own_count), BF16)] * 3 + [(part_shape, BF16)],
        [whole, turned, block[last], sums],
    )
    half_shape = (fsdp // 2, rows, hidden_width)
    sent = call(functools.partial(share_kernel, True), [(half_shape, BF16)] * 3, [block[last], *state, sums])
    kept = call(functools.partial(share_kernel, False), [(half_shape, F32)] * 3, [block[last], *state, sums])

    received = [exchange(array, "fsdp", 1) for array in sent]
    if dp == 2:
        total = 3 * rows
        length = (total // 2 + 15) // 16 * 16
        half = ((length, hidden_width), BF16)
        shares = call(
            functools.partial(split_parts_kernel, 3),
            [half] * fsdp,
            [*kept, *received],
            scratch=[pltpu.VMEM((total, hidden_width), BF16)],
        )
        ready = shares[0]
        landed = [ready]
        for i, share in list(enumerate(shares))[1:]:
            mask, flip = 2 * (i // 2), i % 2
            perm = [(d * fsdp + f, (d ^ flip) * fsdp + (f ^ mask)) for d in range(dp) for f in range(fsdp)]
            landed.append(lax.ppermute(share, ("dp", "fsdp"), perm))
        mine, = call(add_kernel, [half], landed)
        grads = call(
            functools.partial(merge_kernel, 3),
            [((rows, hidden_width), BF16)] * 3,
            [mine, exchange(mine, "dp", 1)],
            outside=True,
            scratch=[pltpu.VMEM((total, hidden_width), BF16)],
        )
    else:
        blocks = call(
            functools.partial(whole_parts_kernel, 3),
            [((3, rows, hidden_width), BF16)] * (fsdp // 2),
            [*kept, *received],
        )
        ready = blocks[0]
        landed = [exchange(blocks[mask], "fsdp", 2 * mask) for mask in range(1, fsdp // 2)]
        mine, = call(add_kernel, [(ready.shape, BF16)], [ready, *landed])
        grads = lax.psum(mine, "dp")

    back = [exchange(part[1], "tensor", 1)]
    for mask in straight:
        arrived = exchange(part[mask ^ 1], "tensor", 1)
        total, = call(middle_kernel, [(part_shape, BF16)], [part[mask], arrived, ready])
        back.append(exchange(total, "tensor", mask))
    part[0], grads = lax.optimization_barrier((part[0], grads))
    mixed, grad_tokens = call(
        functools.partial(rows_sum_kernel, len(back)),
        [((width, own_count), BF16)] * 2,
        [part[0], *back],
        outside=True,
    )
    return mixed.T, grad_tokens.T, grads[0], grads[1], grads[2].T


def solution(mesh):
    token_spec = P(("dp", "fsdp", "tensor"), None)
    return jax.shard_map(
        per_device,
        mesh=mesh,
        in_specs=(token_spec, P("fsdp", "tensor"), P("fsdp", "tensor"), P("tensor", "fsdp"), token_spec),
        out_specs=(token_spec, token_spec, P("fsdp", "tensor"), P("fsdp", "tensor"), P("tensor", "fsdp")),
        check_vma=False,
    )
```

```python
import functools

import jax
import jax.numpy as jnp
from jax import lax
from jax.experimental import pallas as pl
from jax.experimental.pallas import tpu as pltpu
from jax.sharding import PartitionSpec as P

BF16, F32 = jnp.bfloat16, jnp.float32
SCOPED_BYTES = 16 * 1024 * 1024
SPARE = 16


def contract(left, right, left_dim, right_dim):
    return lax.dot_general(left, right, (((left_dim,), (right_dim,)), ((), ())), preferred_element_type=F32)


def exchange(array, axis, mask):
    return lax.ppermute(array, axis, [(i, i ^ mask) for i in range(lax.axis_size(axis))])


def call(body, outs, operands, inside=pltpu.VMEM, outside=False, scratch=()):
    whole = pl.BlockSpec(memory_space=pltpu.VMEM)
    kind = jax.ShapeDtypeStruct if outside else pltpu.VMEM
    return pl.pallas_call(
        body,
        out_shape=[kind(shape, dtype) for shape, dtype in outs],
        in_specs=[pl.BlockSpec(memory_space=inside)] * len(operands),
        out_specs=[whole] * len(outs),
        scratch_shapes=list(scratch),
        cost_estimate=pl.CostEstimate(flops=1, bytes_accessed=1, transcendentals=0),
        compiler_params=pltpu.CompilerParams(vmem_limit_bytes=SCOPED_BYTES),
    )(*[pltpu.with_memory_space_constraint(operand, inside) for operand in operands])


def stack_kernel(counts, *refs):
    arrays, stacks, sems = refs[: sum(counts)], refs[sum(counts):-1], refs[-1]
    places = [(stack, i) for stack, count in zip(stacks, counts) for i in range(count)]
    copies = [
        pltpu.make_async_copy(array, stack.at[i, pl.ds(0, array.shape[0]), :], sems.at[number])
        for number, (array, (stack, i)) in enumerate(zip(arrays, places))
    ]
    for copy in copies:
        copy.start()
    for copy in copies:
        copy.wait()


def stack(*groups, spare=()):
    arrays = [array for group in groups for array in group]
    spares = list(spare) + [0] * (len(groups) - len(spare))
    return call(
        functools.partial(stack_kernel, [len(group) for group in groups]),
        [
            ((len(group), group[0].shape[0] + rows, *group[0].shape[1:]), group[0].dtype)
            for group, rows in zip(groups, spares)
        ],
        arrays,
        inside=pltpu.HBM,
        scratch=[pltpu.SemaphoreType.DMA((len(arrays),))],
    )


def join_kernel(*refs):
    runs, joined = refs[:-1], refs[-1]
    first = 0
    for run in runs:
        joined[first:first + run.shape[0]] = run[...]
        first += run.shape[0]


def assemble_kernel(masks, *refs):
    blocks, (whole, turned) = refs[: len(masks)], refs[len(masks):]
    index = lax.axis_index("fsdp")
    rows = blocks[0].shape[1]
    for mask, block in zip(masks, blocks):
        start = pl.multiple_of((index ^ mask) * rows, 16)
        whole[:, pl.ds(start, rows), :] = block[...]
    for i in range(whole.shape[0]):
        turned[i] = whole[i].T


def forward(turned, rows):
    gate_sum = contract(turned[0], rows, 1, 0)
    up_sum = contract(turned[1], rows, 1, 0)
    sig = 1.0 / (1.0 + jnp.exp(-gate_sum))
    swished = gate_sum * sig
    slopes = up_sum * sig * (1.0 + gate_sum * (1.0 - sig))
    return (swished * up_sum).astype(BF16), swished, slopes


def block_grads(turned, blocks):
    width = turned.shape[2]
    rows, columns = (jnp.concatenate([block[side, :width] for block in blocks], axis=1) for side in range(2))
    hidden, swished, slopes = forward(turned, rows)
    grad_hidden = contract(turned[2], columns, 1, 0)
    grad_gate = (grad_hidden * slopes).astype(BF16)
    grad_up = (grad_hidden * swished).astype(BF16)
    return rows, columns, hidden, grad_gate, grad_up


def token_parts(whole, hidden, grad_gate, grad_up, parts):
    out = contract(whole[2], hidden, 1, 0)
    back = contract(whole[0], grad_gate, 1, 0) + contract(whole[1], grad_up, 1, 0)
    width = out.shape[1] // len(parts)
    rows = out.shape[0]
    for i, part in enumerate(parts):
        part[0, :rows] = out[:, i * width:(i + 1) * width].astype(part.dtype)
        part[1, :rows] = back[:, i * width:(i + 1) * width].astype(part.dtype)
        if part.shape[1] > rows:
            part[:, rows:] = jnp.zeros((2, part.shape[1] - rows, width), part.dtype)


def weight_terms(rows, columns, hidden, grad_gate, grad_up):
    return ((rows, grad_gate), (rows, grad_up), (columns, hidden))


def group_kernel(count, first, whole, turned, *refs):
    blocks, refs = refs[:count], refs[count:]
    before, (after, *parts) = (None, refs) if first else (refs[0], refs[1:])
    rows, columns, hidden, grad_gate, grad_up = block_grads(turned, blocks)
    for i, (left, right) in enumerate(weight_terms(rows, columns, hidden, grad_gate, grad_up)):
        term = contract(left, right, 1, 1)
        after[i] = term if first else before[i] + term
    token_parts(whole, hidden, grad_gate, grad_up, parts)


def last_kernel(turned, block, _, hidden_out, gate_out, up_out):
    _, _, hidden, grad_gate, grad_up = block_grads(turned, [block])
    hidden_out[...], gate_out[...], up_out[...] = hidden, grad_gate, grad_up


def share_terms(pick, block, hidden, grad_gate, grad_up, before, outs):
    pairs, size = outs[0].shape[:2]
    for i, (side, right) in enumerate(((0, grad_gate), (0, grad_up), (1, hidden))):
        for pair in range(pairs):
            start = pl.multiple_of((2 * pair + pick) * size, 16)
            term = contract(block[side, pl.ds(start, size), :], right[...], 1, 1)
            outs[i][pair] = (before[i, pl.ds(start, size), :] + term).astype(outs[i].dtype)


def sent_kernel(block, hidden, grad_gate, grad_up, before, *outs):
    share_terms(1 - lax.axis_index("fsdp") % 2, block, hidden, grad_gate, grad_up, before, outs)


def kept_kernel(whole, block, hidden, grad_gate, grad_up, before, *outs):
    share_terms(lax.axis_index("fsdp") % 2, block, hidden, grad_gate, grad_up, before, outs[:-1])
    token_parts(whole, hidden[...], grad_gate[...], grad_up[...], outs[-1:])


def pair_sums(count, refs):
    kept, received = refs[:count], refs[count:2 * count]
    return lambda i, pair: (kept[i][pair] + received[i][pair].astype(F32)).astype(BF16)


def whole_parts_kernel(count, *refs):
    sums, parts = pair_sums(count, refs), refs[2 * count:]
    index = lax.axis_index("fsdp") // 2
    for mask, part in enumerate(parts):
        for i in range(count):
            part[i] = sums(i, index ^ mask)


def split_parts_kernel(count, *refs):
    sums, parts, rows = pair_sums(count, refs), refs[2 * count:-1], refs[-1]
    index, own = lax.axis_index("fsdp") // 2, lax.axis_index("dp")
    size, length = rows.shape[0] // count, parts[0].shape[0]
    for mask in range(len(parts) // 2):
        for i in range(count):
            rows[i * size:(i + 1) * size] = sums(i, index ^ mask)
        for flip in range(2):
            start = pl.multiple_of((own ^ flip) * (rows.shape[0] - length), 16)
            parts[2 * mask + flip][...] = rows[pl.ds(start, length), :]


def add_kernel(*refs):
    total = refs[0][...].astype(F32)
    for ref in refs[1:-1]:
        total = total + ref[...].astype(F32)
    refs[-1][...] = total.astype(BF16)


def merge_kernel(count, mine, other, *refs):
    outs, rows = refs[:count], refs[count]
    first = lax.axis_index("dp") == 0
    length = mine.shape[0]
    rows[:length] = jnp.where(first, mine[...], other[...])
    rows[rows.shape[0] - length:] = jnp.where(first, other[...], mine[...])
    size = rows.shape[0] // count
    for i, out in enumerate(outs):
        out[...] = rows[i * size:(i + 1) * size]


def middle_kernel(part, received, *refs):
    total = refs[-1]
    total[...] = (part[...] + received[...].astype(F32)).astype(BF16)


def rows_sum_kernel(count, own, *refs):
    received, outs = refs[:count], refs[count:]
    for i, out in enumerate(outs):
        total = own[i]
        for ref in received:
            total = total + ref[i, :out.shape[0]].astype(F32)
        out[...] = total.astype(BF16)


def per_device(tokens, gate_weight, up_weight, down_weight, cotangent):
    tensor, fsdp, dp = (lax.axis_size(axis) for axis in ("tensor", "fsdp", "dp"))
    own_count, width = tokens.shape
    rows, hidden_width = gate_weight.shape

    block, weight = {}, {}
    own_weights = [gate_weight, up_weight, down_weight.T]
    own = [tokens.T, cotangent.T]
    near, block[0] = stack(own, own, spare=[SPARE])
    weight[0], *runs = stack(own_weights, own_weights[:2], own_weights[2:])
    straight = list(range(3, tensor, 2))
    for mask in straight + [1]:
        block[mask] = exchange(near if mask == 1 else block[0], "tensor", mask)
    for mask in straight:
        block[mask], block[1] = lax.optimization_barrier((block[mask], block[1]))
        block[mask ^ 1] = exchange(block[mask], "tensor", 1)
    masks = list(range(fsdp))
    weight[1] = exchange(weight[0], "fsdp", 1)
    for mask in masks[2::2]:
        weight[mask], = call(
            join_kernel, [(weight[0].shape, BF16)], [exchange(run, "fsdp", mask) for run in runs]
        )
        weight[mask + 1] = exchange(weight[mask], "fsdp", 1)
    whole, turned = call(
        functools.partial(assemble_kernel, masks),
        [((3, width, hidden_width), BF16), ((3, hidden_width, width), BF16)],
        [weight[mask] for mask in masks],
    )

    part_shape = (2, width, own_count)
    sums_shape = ((3, width, hidden_width), F32)
    sums, part = [], {}
    forwarded = [mask ^ 1 for mask in straight]
    last = forwarded[-1]
    for group in [[0, 1]] + [[mask] for mask in straight + forwarded[:-1]]:
        kinds = {mask: (part_shape, BF16 if mask % 2 else F32) for mask in group}
        sums, *parts = call(
            functools.partial(group_kernel, len(group), 0 in group),
            [sums_shape] + [kinds[mask] for mask in group],
            [whole, turned] + [block[mask] for mask in group] + ([] if 0 in group else [sums]),
        )
        part.update(zip(group, parts))
    arrived = {}
    for mask in straight:
        part[mask], block[last] = lax.optimization_barrier((part[mask], block[last]))
        arrived[mask] = exchange(part[mask], "tensor", 1)
    state = call(last_kernel, [((hidden_width, own_count), BF16)] * 3, [turned, block[last], sums])
    half_shape = (fsdp // 2, rows, hidden_width)
    sent = call(sent_kernel, [(half_shape, BF16)] * 3, [block[last], *state, sums])
    *kept, part[last] = call(
        kept_kernel, [(half_shape, F32)] * 3 + [(part_shape, F32)], [whole, block[last], *state, sums]
    )

    received = [exchange(array, "fsdp", 1) for array in sent]
    if dp == 2:
        total = 3 * rows
        length = (total // 2 + 15) // 16 * 16
        half = ((length, hidden_width), BF16)
        shares = call(
            functools.partial(split_parts_kernel, 3),
            [half] * fsdp,
            [*kept, *received],
            scratch=[pltpu.VMEM((total, hidden_width), BF16)],
        )
        ready = shares[0]
        landed = [ready]
        for i, share in list(enumerate(shares))[1:]:
            mask, flip = 2 * (i // 2), i % 2
            perm = [(d * fsdp + f, (d ^ flip) * fsdp + (f ^ mask)) for d in range(dp) for f in range(fsdp)]
            landed.append(lax.ppermute(share, ("dp", "fsdp"), perm))
        mine, = call(add_kernel, [half], landed)
        grads = call(
            functools.partial(merge_kernel, 3),
            [((rows, hidden_width), BF16)] * 3,
            [mine, exchange(mine, "dp", 1)],
            outside=True,
            scratch=[pltpu.VMEM((total, hidden_width), BF16)],
        )
    else:
        blocks = call(
            functools.partial(whole_parts_kernel, 3),
            [((3, rows, hidden_width), BF16)] * (fsdp // 2),
            [*kept, *received],
        )
        ready = blocks[0]
        landed = [exchange(blocks[mask], "fsdp", 2 * mask) for mask in range(1, fsdp // 2)]
        mine, = call(add_kernel, [(ready.shape, BF16)], [ready, *landed])
        grads = lax.psum(mine, "dp")

    back = []
    for mask in straight:
        total, = call(middle_kernel, [(part_shape, BF16)], [part[mask ^ 1], arrived[mask], ready])
        part[1], total = lax.optimization_barrier((part[1], total))
        back.append(exchange(total, "tensor", mask ^ 1))
    back.append(exchange(part[1], "tensor", 1))
    part[0], grads = lax.optimization_barrier((part[0], grads))
    mixed, grad_tokens = call(
        functools.partial(rows_sum_kernel, len(back)),
        [((width, own_count), BF16)] * 2,
        [part[0], *back],
        outside=True,
    )
    return mixed.T, grad_tokens.T, grads[0], grads[1], grads[2].T


def solution(mesh):
    token_spec = P(("dp", "fsdp", "tensor"), None)
    return jax.shard_map(
        per_device,
        mesh=mesh,
        in_specs=(token_spec, P("fsdp", "tensor"), P("fsdp", "tensor"), P("tensor", "fsdp"), token_spec),
        out_specs=(token_spec, token_spec, P("fsdp", "tensor"), P("fsdp", "tensor"), P("tensor", "fsdp")),
        check_vma=False,
    )
```

```python
import functools

import jax
import jax.numpy as jnp
from jax import lax
from jax.experimental import pallas as pl
from jax.experimental.pallas import tpu as pltpu
from jax.sharding import PartitionSpec as P

BF16, F32 = jnp.bfloat16, jnp.float32
SCOPED_BYTES = 16 * 1024 * 1024
SPARE = 16


def contract(left, right, left_dim, right_dim):
    return lax.dot_general(left, right, (((left_dim,), (right_dim,)), ((), ())), preferred_element_type=F32)


def exchange(array, axis, mask):
    return lax.ppermute(array, axis, [(i, i ^ mask) for i in range(lax.axis_size(axis))])


def call(body, outs, operands, inside=pltpu.VMEM, outside=False, scratch=()):
    whole = pl.BlockSpec(memory_space=pltpu.VMEM)
    kind = jax.ShapeDtypeStruct if outside else pltpu.VMEM
    return pl.pallas_call(
        body,
        out_shape=[kind(shape, dtype) for shape, dtype in outs],
        in_specs=[pl.BlockSpec(memory_space=inside)] * len(operands),
        out_specs=[whole] * len(outs),
        scratch_shapes=list(scratch),
        cost_estimate=pl.CostEstimate(flops=1, bytes_accessed=1, transcendentals=0),
        compiler_params=pltpu.CompilerParams(vmem_limit_bytes=SCOPED_BYTES),
    )(*[pltpu.with_memory_space_constraint(operand, inside) for operand in operands])


def stack_kernel(counts, *refs):
    arrays, stacks, sems = refs[: sum(counts)], refs[sum(counts):-1], refs[-1]
    places = [(stack, i) for stack, count in zip(stacks, counts) for i in range(count)]
    copies = [
        pltpu.make_async_copy(array, stack.at[i, pl.ds(0, array.shape[0]), :], sems.at[number])
        for number, (array, (stack, i)) in enumerate(zip(arrays, places))
    ]
    for copy in copies:
        copy.start()
    for copy in copies:
        copy.wait()


def stack(*groups, spare=()):
    arrays = [array for group in groups for array in group]
    spares = list(spare) + [0] * (len(groups) - len(spare))
    return call(
        functools.partial(stack_kernel, [len(group) for group in groups]),
        [
            ((len(group), group[0].shape[0] + rows, *group[0].shape[1:]), group[0].dtype)
            for group, rows in zip(groups, spares)
        ],
        arrays,
        inside=pltpu.HBM,
        scratch=[pltpu.SemaphoreType.DMA((len(arrays),))],
    )


def join_kernel(*refs):
    runs, joined = refs[:-1], refs[-1]
    first = 0
    for run in runs:
        joined[first:first + run.shape[0]] = run[...]
        first += run.shape[0]


def assemble_kernel(masks, *refs):
    blocks, (whole, turned) = refs[: len(masks)], refs[len(masks):]
    index = lax.axis_index("fsdp")
    rows = blocks[0].shape[1]
    for mask, block in zip(masks, blocks):
        start = pl.multiple_of((index ^ mask) * rows, 16)
        whole[:, pl.ds(start, rows), :] = block[...]
    for i in range(whole.shape[0]):
        turned[i] = whole[i].T


def forward(turned, rows):
    gate_sum = contract(turned[0], rows, 1, 0)
    up_sum = contract(turned[1], rows, 1, 0)
    sig = 1.0 / (1.0 + jnp.exp(-gate_sum))
    swished = gate_sum * sig
    slopes = up_sum * sig * (1.0 + gate_sum * (1.0 - sig))
    return (swished * up_sum).astype(BF16), swished, slopes


def block_grads(turned, blocks):
    width = turned.shape[2]
    rows, columns = (jnp.concatenate([block[side, :width] for block in blocks], axis=1) for side in range(2))
    hidden, swished, slopes = forward(turned, rows)
    grad_hidden = contract(turned[2], columns, 1, 0)
    grad_gate = (grad_hidden * slopes).astype(BF16)
    grad_up = (grad_hidden * swished).astype(BF16)
    return rows, columns, hidden, grad_gate, grad_up


def token_parts(whole, hidden, grad_gate, grad_up, parts):
    out = contract(whole[2], hidden, 1, 0)
    back = contract(whole[0], grad_gate, 1, 0) + contract(whole[1], grad_up, 1, 0)
    width = out.shape[1] // len(parts)
    rows = out.shape[0]
    for i, part in enumerate(parts):
        part[0, :rows] = out[:, i * width:(i + 1) * width].astype(part.dtype)
        part[1, :rows] = back[:, i * width:(i + 1) * width].astype(part.dtype)
        if part.shape[1] > rows:
            part[:, rows:] = jnp.zeros((2, part.shape[1] - rows, width), part.dtype)


def weight_terms(rows, columns, hidden, grad_gate, grad_up):
    return ((rows, grad_gate), (rows, grad_up), (columns, hidden))


def group_kernel(count, first, whole, turned, *refs):
    blocks, refs = refs[:count], refs[count:]
    before, (after, *parts) = (None, refs) if first else (refs[0], refs[1:])
    rows, columns, hidden, grad_gate, grad_up = block_grads(turned, blocks)
    for i, (left, right) in enumerate(weight_terms(rows, columns, hidden, grad_gate, grad_up)):
        term = contract(left, right, 1, 1)
        after[i] = term if first else before[i] + term
    token_parts(whole, hidden, grad_gate, grad_up, parts)


def last_kernel(turned, block, _, hidden_out, gate_out, up_out):
    _, _, hidden, grad_gate, grad_up = block_grads(turned, [block])
    hidden_out[...], gate_out[...], up_out[...] = hidden, grad_gate, grad_up


def share_terms(pick, block, hidden, grad_gate, grad_up, before, outs):
    pairs, size = outs[0].shape[:2]
    for i, (side, right) in enumerate(((0, grad_gate), (0, grad_up), (1, hidden))):
        for pair in range(pairs):
            start = pl.multiple_of((2 * pair + pick) * size, 16)
            term = contract(block[side, pl.ds(start, size), :], right[...], 1, 1)
            outs[i][pair] = (before[i, pl.ds(start, size), :] + term).astype(outs[i].dtype)


def sent_kernel(block, hidden, grad_gate, grad_up, before, *outs):
    share_terms(1 - lax.axis_index("fsdp") % 2, block, hidden, grad_gate, grad_up, before, outs)


def kept_kernel(whole, block, hidden, grad_gate, grad_up, before, *outs):
    share_terms(lax.axis_index("fsdp") % 2, block, hidden, grad_gate, grad_up, before, outs[:-1])
    token_parts(whole, hidden[...], grad_gate[...], grad_up[...], outs[-1:])


def pair_sums(count, refs):
    kept, received = refs[:count], refs[count:2 * count]
    return lambda i, pair: (kept[i][pair] + received[i][pair].astype(F32)).astype(BF16)


def whole_parts_kernel(count, *refs):
    sums, parts = pair_sums(count, refs), refs[2 * count:]
    index = lax.axis_index("fsdp") // 2
    for mask, part in enumerate(parts):
        for i in range(count):
            part[i] = sums(i, index ^ mask)


def split_parts_kernel(count, *refs):
    sums, parts, rows = pair_sums(count, refs), refs[2 * count:-1], refs[-1]
    index, own = lax.axis_index("fsdp") // 2, lax.axis_index("dp")
    size, length = rows.shape[0] // count, parts[0].shape[0]
    for mask in range(len(parts) // 2):
        for i in range(count):
            rows[i * size:(i + 1) * size] = sums(i, index ^ mask)
        for flip in range(2):
            start = pl.multiple_of((own ^ flip) * (rows.shape[0] - length), 16)
            parts[2 * mask + flip][...] = rows[pl.ds(start, length), :]


def add_kernel(*refs):
    total = refs[0][...].astype(F32)
    for ref in refs[1:-1]:
        total = total + ref[...].astype(F32)
    refs[-1][...] = total.astype(BF16)


def merge_kernel(count, mine, other, *refs):
    outs, rows = refs[:count], refs[count]
    first = lax.axis_index("dp") == 0
    length = mine.shape[0]
    rows[:length] = jnp.where(first, mine[...], other[...])
    rows[rows.shape[0] - length:] = jnp.where(first, other[...], mine[...])
    size = rows.shape[0] // count
    for i, out in enumerate(outs):
        out[...] = rows[i * size:(i + 1) * size]


def middle_kernel(part, received, *refs):
    total = refs[-1]
    total[...] = (part[...] + received[...].astype(F32)).astype(BF16)


def rows_sum_kernel(count, own, *refs):
    received, outs = refs[:count], refs[count:]
    for i, out in enumerate(outs):
        total = own[i]
        for ref in received:
            total = total + ref[i, :out.shape[0]].astype(F32)
        out[...] = total.astype(BF16)


def per_device(tokens, gate_weight, up_weight, down_weight, cotangent):
    tensor, fsdp, dp = (lax.axis_size(axis) for axis in ("tensor", "fsdp", "dp"))
    own_count, width = tokens.shape
    rows, hidden_width = gate_weight.shape

    block, weight = {}, {}
    own_weights = [gate_weight, up_weight, down_weight.T]
    own = [tokens.T, cotangent.T]
    near, block[0] = stack(own, own, spare=[SPARE])
    weight[0], *runs = stack(own_weights, own_weights[:2], own_weights[2:])
    straight = list(range(3, tensor, 2))
    for mask in straight + [1]:
        block[mask] = exchange(near if mask == 1 else block[0], "tensor", mask)
    for mask in straight:
        block[mask], block[1] = lax.optimization_barrier((block[mask], block[1]))
        block[mask ^ 1] = exchange(block[mask], "tensor", 1)
    masks = list(range(fsdp))
    weight[1] = exchange(weight[0], "fsdp", 1)
    for mask in masks[2::2]:
        weight[mask], = call(
            join_kernel, [(weight[0].shape, BF16)], [exchange(run, "fsdp", mask) for run in runs]
        )
        weight[mask + 1] = exchange(weight[mask], "fsdp", 1)
    whole, turned = call(
        functools.partial(assemble_kernel, masks),
        [((3, width, hidden_width), BF16), ((3, hidden_width, width), BF16)],
        [weight[mask] for mask in masks],
    )

    part_shape = (2, width, own_count)
    sums_shape = ((3, width, hidden_width), F32)
    sums, part = [], {}
    forwarded = [mask ^ 1 for mask in straight]
    last = forwarded[-1]
    for group in [[0, 1]] + [[mask] for mask in straight + forwarded[:-1]]:
        kinds = {mask: (part_shape, BF16 if mask % 2 else F32) for mask in group}
        sums, *parts = call(
            functools.partial(group_kernel, len(group), 0 in group),
            [sums_shape] + [kinds[mask] for mask in group],
            [whole, turned] + [block[mask] for mask in group] + ([] if 0 in group else [sums]),
        )
        part.update(zip(group, parts))
    arrived = {mask: exchange(part[mask], "tensor", 1) for mask in straight}
    state = call(last_kernel, [((hidden_width, own_count), BF16)] * 3, [turned, block[last], sums])
    half_shape = (fsdp // 2, rows, hidden_width)
    sent = call(sent_kernel, [(half_shape, BF16)] * 3, [block[last], *state, sums])
    *kept, part[last] = call(
        kept_kernel, [(half_shape, F32)] * 3 + [(part_shape, F32)], [whole, block[last], *state, sums]
    )

    received = [exchange(array, "fsdp", 1) for array in sent]
    if dp == 2:
        total = 3 * rows
        length = (total // 2 + 15) // 16 * 16
        half = ((length, hidden_width), BF16)
        shares = call(
            functools.partial(split_parts_kernel, 3),
            [half] * fsdp,
            [*kept, *received],
            scratch=[pltpu.VMEM((total, hidden_width), BF16)],
        )
        ready = shares[0]
        landed = [ready]
        for i, share in list(enumerate(shares))[1:]:
            mask, flip = 2 * (i // 2), i % 2
            perm = [(d * fsdp + f, (d ^ flip) * fsdp + (f ^ mask)) for d in range(dp) for f in range(fsdp)]
            landed.append(lax.ppermute(share, ("dp", "fsdp"), perm))
        mine, = call(add_kernel, [half], landed)
        grads = call(
            functools.partial(merge_kernel, 3),
            [((rows, hidden_width), BF16)] * 3,
            [mine, exchange(mine, "dp", 1)],
            outside=True,
            scratch=[pltpu.VMEM((total, hidden_width), BF16)],
        )
    else:
        blocks = call(
            functools.partial(whole_parts_kernel, 3),
            [((3, rows, hidden_width), BF16)] * (fsdp // 2),
            [*kept, *received],
        )
        ready = blocks[0]
        landed = [exchange(blocks[mask], "fsdp", 2 * mask) for mask in range(1, fsdp // 2)]
        mine, = call(add_kernel, [(ready.shape, BF16)], [ready, *landed])
        grads = lax.psum(mine, "dp")

    back = []
    for mask in straight:
        total, = call(middle_kernel, [(part_shape, BF16)], [part[mask ^ 1], arrived[mask], ready])
        part[1], total = lax.optimization_barrier((part[1], total))
        back.append(exchange(total, "tensor", mask ^ 1))
    back.append(exchange(part[1], "tensor", 1))
    part[0], grads = lax.optimization_barrier((part[0], grads))
    mixed, grad_tokens = call(
        functools.partial(rows_sum_kernel, len(back)),
        [((width, own_count), BF16)] * 2,
        [part[0], *back],
        outside=True,
    )
    return mixed.T, grad_tokens.T, grads[0], grads[1], grads[2].T


def solution(mesh):
    token_spec = P(("dp", "fsdp", "tensor"), None)
    return jax.shard_map(
        per_device,
        mesh=mesh,
        in_specs=(token_spec, P("fsdp", "tensor"), P("fsdp", "tensor"), P("tensor", "fsdp"), token_spec),
        out_specs=(token_spec, token_spec, P("fsdp", "tensor"), P("fsdp", "tensor"), P("tensor", "fsdp")),
        check_vma=False,
    )
```

```python
import functools

import jax
import jax.numpy as jnp
from jax import lax
from jax.experimental import pallas as pl
from jax.experimental.pallas import tpu as pltpu
from jax.sharding import PartitionSpec as P

BF16, F32 = jnp.bfloat16, jnp.float32
SCOPED_BYTES = 16 * 1024 * 1024
SPARE = 16


def contract(left, right, left_dim, right_dim):
    return lax.dot_general(left, right, (((left_dim,), (right_dim,)), ((), ())), preferred_element_type=F32)


def exchange(array, axis, mask):
    return lax.ppermute(array, axis, [(i, i ^ mask) for i in range(lax.axis_size(axis))])


def call(body, outs, operands, inside=pltpu.VMEM, outside=False, scratch=()):
    whole = pl.BlockSpec(memory_space=pltpu.VMEM)
    kind = jax.ShapeDtypeStruct if outside else pltpu.VMEM
    return pl.pallas_call(
        body,
        out_shape=[kind(shape, dtype) for shape, dtype in outs],
        in_specs=[pl.BlockSpec(memory_space=inside)] * len(operands),
        out_specs=[whole] * len(outs),
        scratch_shapes=list(scratch),
        cost_estimate=pl.CostEstimate(flops=1, bytes_accessed=1, transcendentals=0),
        compiler_params=pltpu.CompilerParams(vmem_limit_bytes=SCOPED_BYTES),
    )(*[pltpu.with_memory_space_constraint(operand, inside) for operand in operands])


def stack_kernel(counts, twin, *refs):
    arrays, sems = refs[: sum(counts)], refs[-1]
    stacks = refs[len(arrays):len(arrays) + len(counts)]
    places = [stack.at[i] for stack, count in zip(stacks, counts) for i in range(count)]
    copies = [pltpu.make_async_copy(array, place, sems.at[i]) for i, (array, place) in enumerate(zip(arrays, places))]
    for copy in copies:
        copy.start()
    for copy in copies:
        copy.wait()
    if twin:
        refs[-2][:, :stacks[0].shape[1]] = stacks[0][...]


def stack(*groups, spare=0):
    arrays = [array for group in groups for array in group]
    outs = [((len(group), *group[0].shape), group[0].dtype) for group in groups]
    if spare:
        (count, rows, columns), dtype = outs[0]
        outs.append(((count, rows + spare, columns), dtype))
    return call(
        functools.partial(stack_kernel, [len(group) for group in groups], bool(spare)),
        outs,
        arrays,
        inside=pltpu.HBM,
        scratch=[pltpu.SemaphoreType.DMA((len(arrays),))],
    )


def join_kernel(*refs):
    runs, joined = refs[:-1], refs[-1]
    first = 0
    for run in runs:
        joined[first:first + run.shape[0]] = run[...]
        first += run.shape[0]


def assemble_kernel(masks, *refs):
    blocks, (whole, turned) = refs[: len(masks)], refs[len(masks):]
    index = lax.axis_index("fsdp")
    rows = blocks[0].shape[1]
    for mask, block in zip(masks, blocks):
        start = pl.multiple_of((index ^ mask) * rows, 16)
        whole[:, pl.ds(start, rows), :] = block[...]
    for i in range(whole.shape[0]):
        turned[i] = whole[i].T


def forward(turned, rows):
    gate_sum = contract(turned[0], rows, 1, 0)
    up_sum = contract(turned[1], rows, 1, 0)
    sig = 1.0 / (1.0 + jnp.exp(-gate_sum))
    swished = gate_sum * sig
    slopes = up_sum * sig * (1.0 + gate_sum * (1.0 - sig))
    return (swished * up_sum).astype(BF16), swished, slopes


def block_grads(turned, blocks):
    width = turned.shape[2]
    rows, columns = (jnp.concatenate([block[side, :width] for block in blocks], axis=1) for side in range(2))
    hidden, swished, slopes = forward(turned, rows)
    grad_hidden = contract(turned[2], columns, 1, 0)
    grad_gate = (grad_hidden * slopes).astype(BF16)
    grad_up = (grad_hidden * swished).astype(BF16)
    return rows, columns, hidden, grad_gate, grad_up


def token_parts(whole, hidden, grad_gate, grad_up, parts):
    out = contract(whole[2], hidden, 1, 0)
    back = contract(whole[0], grad_gate, 1, 0) + contract(whole[1], grad_up, 1, 0)
    width = out.shape[1] // len(parts)
    rows = out.shape[0]
    for i, part in enumerate(parts):
        part[0, :rows] = out[:, i * width:(i + 1) * width].astype(part.dtype)
        part[1, :rows] = back[:, i * width:(i + 1) * width].astype(part.dtype)
        if part.shape[1] > rows:
            part[:, rows:] = jnp.zeros((2, part.shape[1] - rows, width), part.dtype)


def weight_terms(rows, columns, hidden, grad_gate, grad_up):
    return ((rows, grad_gate), (rows, grad_up), (columns, hidden))


def group_kernel(count, first, whole, turned, *refs):
    blocks, refs = refs[:count], refs[count:]
    before, (after, *parts) = (None, refs) if first else (refs[0], refs[1:])
    rows, columns, hidden, grad_gate, grad_up = block_grads(turned, blocks)
    for i, (left, right) in enumerate(weight_terms(rows, columns, hidden, grad_gate, grad_up)):
        term = contract(left, right, 1, 1)
        after[i] = term if first else before[i] + term
    token_parts(whole, hidden, grad_gate, grad_up, parts)


def share_terms(pick, block, hidden, grad_gate, grad_up, before, outs):
    pairs, size = outs[0].shape[:2]
    for i, (side, right) in enumerate(((0, grad_gate), (0, grad_up), (1, hidden))):
        for pair in range(pairs):
            start = pl.multiple_of((2 * pair + pick) * size, 16)
            term = contract(block[side, pl.ds(start, size), :], right, 1, 1)
            outs[i][pair] = (before[i, pl.ds(start, size), :] + term).astype(outs[i].dtype)


def last_kernel(turned, block, before, hidden_out, gate_out, up_out, *outs):
    _, _, hidden, grad_gate, grad_up = block_grads(turned, [block])
    hidden_out[...], gate_out[...], up_out[...] = hidden, grad_gate, grad_up
    share_terms(1 - lax.axis_index("fsdp") % 2, block, hidden, grad_gate, grad_up, before, outs)


def kept_kernel(whole, block, hidden, grad_gate, grad_up, before, *outs):
    values = hidden[...], grad_gate[...], grad_up[...]
    share_terms(lax.axis_index("fsdp") % 2, block, *values, before, outs[:-1])
    token_parts(whole, *values, outs[-1:])


def pair_sums(count, refs):
    kept, received = refs[:count], refs[count:2 * count]
    return lambda i, pair: (kept[i][pair] + received[i][pair].astype(F32)).astype(BF16)


def whole_parts_kernel(count, *refs):
    sums, parts = pair_sums(count, refs), refs[2 * count:]
    index = lax.axis_index("fsdp") // 2
    for mask, part in enumerate(parts):
        for i in range(count):
            part[i] = sums(i, index ^ mask)


def split_parts_kernel(count, *refs):
    sums, parts, rows = pair_sums(count, refs), refs[2 * count:-1], refs[-1]
    index, own = lax.axis_index("fsdp") // 2, lax.axis_index("dp")
    size, length = rows.shape[0] // count, parts[0].shape[0]
    for mask in range(len(parts) // 2):
        for i in range(count):
            rows[i * size:(i + 1) * size] = sums(i, index ^ mask)
        for flip in range(2):
            start = pl.multiple_of((own ^ flip) * (rows.shape[0] - length), 16)
            parts[2 * mask + flip][...] = rows[pl.ds(start, length), :]


def add_kernel(*refs):
    total = refs[0][...].astype(F32)
    for ref in refs[1:-1]:
        total = total + ref[...].astype(F32)
    refs[-1][...] = total.astype(BF16)


def merge_kernel(count, mine, other, *refs):
    outs, rows = refs[:count], refs[count]
    first = lax.axis_index("dp") == 0
    length = mine.shape[0]
    rows[:length] = jnp.where(first, mine[...], other[...])
    rows[rows.shape[0] - length:] = jnp.where(first, other[...], mine[...])
    size = rows.shape[0] // count
    for i, out in enumerate(outs):
        out[...] = rows[i * size:(i + 1) * size]


def middle_kernel(part, received, *refs):
    total = refs[-1]
    total[...] = (part[...] + received[...].astype(F32)).astype(BF16)


def rows_sum_kernel(count, own, *refs):
    received, outs = refs[:count], refs[count:]
    for i, out in enumerate(outs):
        total = own[i]
        for ref in received:
            total = total + ref[i, :out.shape[0]].astype(F32)
        out[...] = total.astype(BF16)


def per_device(tokens, gate_weight, up_weight, down_weight, cotangent):
    tensor, fsdp, dp = (lax.axis_size(axis) for axis in ("tensor", "fsdp", "dp"))
    own_count, width = tokens.shape
    rows, hidden_width = gate_weight.shape

    block, weight = {}, {}
    own_weights = [gate_weight, up_weight, down_weight.T]
    block[0], near = stack([tokens.T, cotangent.T], spare=SPARE)
    weight[0], *runs = stack(own_weights, own_weights[:2], own_weights[2:])
    straight = list(range(3, tensor, 2))
    for mask in straight + [1]:
        block[mask] = exchange(near if mask == 1 else block[0], "tensor", mask)
    for mask in straight:
        block[mask], block[1] = lax.optimization_barrier((block[mask], block[1]))
        block[mask ^ 1] = exchange(block[mask], "tensor", 1)
    masks = list(range(fsdp))
    weight[1] = exchange(weight[0], "fsdp", 1)
    for mask in masks[2::2]:
        weight[mask], = call(
            join_kernel, [(weight[0].shape, BF16)], [exchange(run, "fsdp", mask) for run in runs]
        )
        weight[mask + 1] = exchange(weight[mask], "fsdp", 1)
    whole, turned = call(
        functools.partial(assemble_kernel, masks),
        [((3, width, hidden_width), BF16), ((3, hidden_width, width), BF16)],
        [weight[mask] for mask in masks],
    )

    part_shape = (2, width, own_count)
    sums_shape = ((3, width, hidden_width), F32)
    sums, part = [], {}
    forwarded = [mask ^ 1 for mask in straight]
    last = forwarded[-1]
    for group in [[0, 1]] + [[mask] for mask in straight + forwarded[:-1]]:
        kinds = {mask: (part_shape, BF16 if mask % 2 else F32) for mask in group}
        sums, *parts = call(
            functools.partial(group_kernel, len(group), 0 in group),
            [sums_shape] + [kinds[mask] for mask in group],
            [whole, turned] + [block[mask] for mask in group] + ([] if 0 in group else [sums]),
        )
        part.update(zip(group, parts))
    arrived = {}
    for mask in straight:
        part[mask], block[last] = lax.optimization_barrier((part[mask], block[last]))
        arrived[mask] = exchange(part[mask], "tensor", 1)
    half_shape = (fsdp // 2, rows, hidden_width)
    results = call(
        last_kernel,
        [((hidden_width, own_count), BF16)] * 3 + [(half_shape, BF16)] * 3,
        [turned, block[last], sums],
    )
    state, sent = results[:3], results[3:]
    *kept, part[last] = call(
        kept_kernel, [(half_shape, F32)] * 3 + [(part_shape, F32)], [whole, block[last], *state, sums]
    )

    received = [exchange(array, "fsdp", 1) for array in sent]
    if dp == 2:
        total = 3 * rows
        length = (total // 2 + 15) // 16 * 16
        half = ((length, hidden_width), BF16)
        shares = call(
            functools.partial(split_parts_kernel, 3),
            [half] * fsdp,
            [*kept, *received],
            scratch=[pltpu.VMEM((total, hidden_width), BF16)],
        )
        ready = shares[0]
        landed = [ready]
        for i, share in list(enumerate(shares))[1:]:
            mask, flip = 2 * (i // 2), i % 2
            perm = [(d * fsdp + f, (d ^ flip) * fsdp + (f ^ mask)) for d in range(dp) for f in range(fsdp)]
            landed.append(lax.ppermute(share, ("dp", "fsdp"), perm))
        mine, = call(add_kernel, [half], landed)
        grads = call(
            functools.partial(merge_kernel, 3),
            [((rows, hidden_width), BF16)] * 3,
            [mine, exchange(mine, "dp", 1)],
            outside=True,
            scratch=[pltpu.VMEM((total, hidden_width), BF16)],
        )
    else:
        blocks = call(
            functools.partial(whole_parts_kernel, 3),
            [((3, rows, hidden_width), BF16)] * (fsdp // 2),
            [*kept, *received],
        )
        ready = blocks[0]
        landed = [exchange(blocks[mask], "fsdp", 2 * mask) for mask in range(1, fsdp // 2)]
        mine, = call(add_kernel, [(ready.shape, BF16)], [ready, *landed])
        grads = lax.psum(mine, "dp")

    back = []
    for mask in straight:
        total, = call(middle_kernel, [(part_shape, BF16)], [part[mask ^ 1], arrived[mask], ready])
        part[1], total = lax.optimization_barrier((part[1], total))
        back.append(exchange(total, "tensor", mask ^ 1))
    back.append(exchange(part[1], "tensor", 1))
    part[0], grads = lax.optimization_barrier((part[0], grads))
    mixed, grad_tokens = call(
        functools.partial(rows_sum_kernel, len(back)),
        [((width, own_count), BF16)] * 2,
        [part[0], *back],
        outside=True,
    )
    return mixed.T, grad_tokens.T, grads[0], grads[1], grads[2].T


def solution(mesh):
    token_spec = P(("dp", "fsdp", "tensor"), None)
    return jax.shard_map(
        per_device,
        mesh=mesh,
        in_specs=(token_spec, P("fsdp", "tensor"), P("fsdp", "tensor"), P("tensor", "fsdp"), token_spec),
        out_specs=(token_spec, token_spec, P("fsdp", "tensor"), P("fsdp", "tensor"), P("tensor", "fsdp")),
        check_vma=False,
    )
```

```python
import functools

import jax
import jax.numpy as jnp
from jax import lax
from jax.experimental import pallas as pl
from jax.experimental.pallas import tpu as pltpu
from jax.sharding import PartitionSpec as P

BF16, F32 = jnp.bfloat16, jnp.float32
SCOPED_BYTES = 16 * 1024 * 1024
SPARE = 16


def contract(left, right, left_dim, right_dim):
    return lax.dot_general(left, right, (((left_dim,), (right_dim,)), ((), ())), preferred_element_type=F32)


def exchange(array, axis, mask):
    return lax.ppermute(array, axis, [(i, i ^ mask) for i in range(lax.axis_size(axis))])


def call(body, outs, operands, inside=pltpu.VMEM, outside=False, scratch=()):
    whole = pl.BlockSpec(memory_space=pltpu.VMEM)
    kind = jax.ShapeDtypeStruct if outside else pltpu.VMEM
    return pl.pallas_call(
        body,
        out_shape=[kind(shape, dtype) for shape, dtype in outs],
        in_specs=[pl.BlockSpec(memory_space=inside)] * len(operands),
        out_specs=[whole] * len(outs),
        scratch_shapes=list(scratch),
        cost_estimate=pl.CostEstimate(flops=1, bytes_accessed=1, transcendentals=0),
        compiler_params=pltpu.CompilerParams(vmem_limit_bytes=SCOPED_BYTES),
    )(*[pltpu.with_memory_space_constraint(operand, inside) for operand in operands])


def stack_kernel(counts, twin, *refs):
    arrays, sems = refs[: sum(counts)], refs[-1]
    stacks = refs[len(arrays):len(arrays) + len(counts)]
    places = [stack.at[i] for stack, count in zip(stacks, counts) for i in range(count)]
    copies = [pltpu.make_async_copy(array, place, sems.at[i]) for i, (array, place) in enumerate(zip(arrays, places))]
    for copy in copies:
        copy.start()
    for copy in copies:
        copy.wait()
    if twin:
        refs[-2][:, :stacks[0].shape[1]] = stacks[0][...]


def pieces_kernel(*refs):
    arrays, (stacked, top, bottom, sems) = refs[:-4], refs[-4:]
    copies = [pltpu.make_async_copy(array, stacked.at[i], sems.at[i]) for i, array in enumerate(arrays)]
    for copy in copies:
        copy.start()
    for copy in copies:
        copy.wait()
    length = top.shape[1]
    top[...] = stacked[:, :length]
    bottom[...] = stacked[:, stacked.shape[1] - length:]


def stack(*groups, spare=0):
    arrays = [array for group in groups for array in group]
    outs = [((len(group), *group[0].shape), group[0].dtype) for group in groups]
    if spare:
        (count, rows, columns), dtype = outs[0]
        outs.append(((count, rows + spare, columns), dtype))
    return call(
        functools.partial(stack_kernel, [len(group) for group in groups], bool(spare)),
        outs,
        arrays,
        inside=pltpu.HBM,
        scratch=[pltpu.SemaphoreType.DMA((len(arrays),))],
    )


def join_kernel(top, bottom, joined):
    length = top.shape[1]
    joined[:, :length] = top[...]
    joined[:, joined.shape[1] - length:] = bottom[...]


def assemble_kernel(masks, *refs):
    blocks, (whole, turned) = refs[: len(masks)], refs[len(masks):]
    index = lax.axis_index("fsdp")
    rows = blocks[0].shape[1]
    for mask, block in zip(masks, blocks):
        start = pl.multiple_of((index ^ mask) * rows, 16)
        whole[:, pl.ds(start, rows), :] = block[...]
    for i in range(whole.shape[0]):
        turned[i] = whole[i].T


def forward(turned, rows):
    gate_sum = contract(turned[0], rows, 1, 0)
    up_sum = contract(turned[1], rows, 1, 0)
    sig = 1.0 / (1.0 + jnp.exp(-gate_sum))
    swished = gate_sum * sig
    slopes = up_sum * sig * (1.0 + gate_sum * (1.0 - sig))
    return (swished * up_sum).astype(BF16), swished, slopes


def block_grads(turned, rows, columns):
    hidden, swished, slopes = forward(turned, rows)
    grad_hidden = contract(turned[2], columns, 1, 0)
    return hidden, (grad_hidden * slopes).astype(BF16), (grad_hidden * swished).astype(BF16)


def token_parts(whole, hidden, grad_gate, grad_up, parts):
    out = contract(whole[2], hidden, 1, 0)
    back = contract(whole[0], grad_gate, 1, 0) + contract(whole[1], grad_up, 1, 0)
    width = out.shape[1] // len(parts)
    rows = out.shape[0]
    for i, part in enumerate(parts):
        part[0, :rows] = out[:, i * width:(i + 1) * width].astype(part.dtype)
        part[1, :rows] = back[:, i * width:(i + 1) * width].astype(part.dtype)
        if part.shape[1] > rows:
            part[:, rows:] = jnp.zeros((2, part.shape[1] - rows, width), part.dtype)


def weight_terms(rows, columns, hidden, grad_gate, grad_up):
    return ((rows, grad_gate), (rows, grad_up), (columns, hidden))


def group_kernel(count, first, whole, turned, *refs):
    blocks, refs = refs[:count], refs[count:]
    before, (after, *parts) = (None, refs) if first else (refs[0], refs[1:])
    width = turned.shape[2]
    rows, columns = (jnp.concatenate([block[side, :width] for block in blocks], axis=1) for side in range(2))
    hidden, grad_gate, grad_up = block_grads(turned, rows, columns)
    for i, (left, right) in enumerate(weight_terms(rows, columns, hidden, grad_gate, grad_up)):
        term = contract(left, right, 1, 1)
        after[i] = term if first else before[i] + term
    token_parts(whole, hidden, grad_gate, grad_up, parts)


def share_terms(pick, tokens, cotangent, hidden, grad_gate, grad_up, before, outs):
    pairs, size = outs[0].shape[:2]
    for i, (left, right) in enumerate(((tokens, grad_gate), (tokens, grad_up), (cotangent, hidden))):
        for pair in range(pairs):
            start = pl.multiple_of((2 * pair + pick) * size, 16)
            term = contract(left[pl.ds(start, size), :], right, 1, 1)
            outs[i][pair] = (before[i, pl.ds(start, size), :] + term).astype(outs[i].dtype)


def last_kernel(turned, tokens, cotangent, before, hidden_out, gate_out, up_out, *outs):
    hidden, grad_gate, grad_up = block_grads(turned, tokens[...], cotangent[...])
    hidden_out[...], gate_out[...], up_out[...] = hidden, grad_gate, grad_up
    share_terms(1 - lax.axis_index("fsdp") % 2, tokens, cotangent, hidden, grad_gate, grad_up, before, outs)


def kept_kernel(whole, tokens, cotangent, hidden, grad_gate, grad_up, before, *outs):
    values = hidden[...], grad_gate[...], grad_up[...]
    share_terms(lax.axis_index("fsdp") % 2, tokens, cotangent, *values, before, outs[:-1])
    token_parts(whole, *values, outs[-1:])


def pair_sums(count, refs):
    kept, received = refs[:count], refs[count:2 * count]
    return lambda i, pair: (kept[i][pair] + received[i][pair].astype(F32)).astype(BF16)


def whole_parts_kernel(count, *refs):
    sums, parts = pair_sums(count, refs), refs[2 * count:]
    index = lax.axis_index("fsdp") // 2
    for mask, part in enumerate(parts):
        for i in range(count):
            part[i] = sums(i, index ^ mask)


def split_parts_kernel(count, *refs):
    sums, parts, rows = pair_sums(count, refs), refs[2 * count:-1], refs[-1]
    index, own = lax.axis_index("fsdp") // 2, lax.axis_index("dp")
    size, length = rows.shape[0] // count, parts[0].shape[0]
    for mask in range(len(parts) // 2):
        for i in range(count):
            rows[i * size:(i + 1) * size] = sums(i, index ^ mask)
        for flip in range(2):
            start = pl.multiple_of((own ^ flip) * (rows.shape[0] - length), 16)
            parts[2 * mask + flip][...] = rows[pl.ds(start, length), :]


def add_kernel(*refs):
    total = refs[0][...].astype(F32)
    for ref in refs[1:-1]:
        total = total + ref[...].astype(F32)
    refs[-1][...] = total.astype(BF16)


def merge_kernel(count, mine, other, *refs):
    outs, rows = refs[:count], refs[count]
    first = lax.axis_index("dp") == 0
    length = mine.shape[0]
    rows[:length] = jnp.where(first, mine[...], other[...])
    rows[rows.shape[0] - length:] = jnp.where(first, other[...], mine[...])
    size = rows.shape[0] // count
    for i, out in enumerate(outs):
        out[...] = rows[i * size:(i + 1) * size]


def middle_kernel(part, received, *refs):
    total = refs[-1]
    total[...] = (part[...] + received[...].astype(F32)).astype(BF16)


def rows_sum_kernel(count, own, *refs):
    received, outs = refs[:count], refs[count:]
    for i, out in enumerate(outs):
        total = own[i]
        for ref in received:
            total = total + ref[i, :out.shape[0]].astype(F32)
        out[...] = total.astype(BF16)


def per_device(tokens, gate_weight, up_weight, down_weight, cotangent):
    tensor, fsdp, dp = (lax.axis_size(axis) for axis in ("tensor", "fsdp", "dp"))
    own_count, width = tokens.shape
    rows, hidden_width = gate_weight.shape

    block, weight = {}, {}
    own_weights = [gate_weight, up_weight, down_weight.T]
    block[0], near = stack([tokens.T, cotangent.T], spare=SPARE)
    piece = (rows // 2 + 15) // 16 * 16
    weight[0], *runs = call(
        pieces_kernel,
        [((3, length, hidden_width), BF16) for length in (rows, piece, piece)],
        own_weights,
        inside=pltpu.HBM,
        scratch=[pltpu.SemaphoreType.DMA((3,))],
    )
    straight = list(range(3, tensor, 2))
    for mask in straight + [1]:
        block[mask] = exchange(near if mask == 1 else block[0], "tensor", mask)
    for mask in straight:
        block[mask], block[1] = lax.optimization_barrier((block[mask], block[1]))
        if mask != straight[-1]:
            block[mask ^ 1] = exchange(block[mask], "tensor", 1)
    final = [exchange(block[straight[-1]][side], "tensor", 1) for side in range(2)]
    masks = list(range(fsdp))
    weight[1] = exchange(weight[0], "fsdp", 1)
    for mask in masks[2::2]:
        landed = [exchange(run, "fsdp", mask) for run in runs]
        weight[mask], = call(join_kernel, [(weight[0].shape, BF16)], landed)
        weight[mask + 1], = call(
            join_kernel, [(weight[0].shape, BF16)], [exchange(run, "fsdp", 1) for run in landed]
        )
    whole, turned = call(
        functools.partial(assemble_kernel, masks),
        [((3, width, hidden_width), BF16), ((3, hidden_width, width), BF16)],
        [weight[mask] for mask in masks],
    )

    part_shape = (2, width, own_count)
    sums_shape = ((3, width, hidden_width), F32)
    sums, part = [], {}
    forwarded = [mask ^ 1 for mask in straight]
    last = forwarded[-1]
    for group in [[0, 1]] + [[mask] for mask in straight + forwarded[:-1]]:
        kinds = {mask: (part_shape, BF16 if mask % 2 else F32) for mask in group}
        sums, *parts = call(
            functools.partial(group_kernel, len(group), 0 in group),
            [sums_shape] + [kinds[mask] for mask in group],
            [whole, turned] + [block[mask] for mask in group] + ([] if 0 in group else [sums]),
        )
        part.update(zip(group, parts))
    arrived = {}
    for mask in straight:
        part[mask], final = lax.optimization_barrier((part[mask], final))
        arrived[mask] = exchange(part[mask], "tensor", 1)
    half_shape = (fsdp // 2, rows, hidden_width)
    results = call(
        last_kernel,
        [((hidden_width, own_count), BF16)] * 3 + [(half_shape, BF16)] * 3,
        [turned, *final, sums],
    )
    state, sent = results[:3], results[3:]
    *kept, part[last] = call(
        kept_kernel, [(half_shape, F32)] * 3 + [(part_shape, F32)], [whole, *final, *state, sums]
    )

    received = [exchange(array, "fsdp", 1) for array in sent]
    if dp == 2:
        total = 3 * rows
        length = (total // 2 + 15) // 16 * 16
        half = ((length, hidden_width), BF16)
        shares = call(
            functools.partial(split_parts_kernel, 3),
            [half] * fsdp,
            [*kept, *received],
            scratch=[pltpu.VMEM((total, hidden_width), BF16)],
        )
        ready = shares[0]
        landed = [ready]
        for i, share in list(enumerate(shares))[1:]:
            mask, flip = 2 * (i // 2), i % 2
            perm = [(d * fsdp + f, (d ^ flip) * fsdp + (f ^ mask)) for d in range(dp) for f in range(fsdp)]
            landed.append(lax.ppermute(share, ("dp", "fsdp"), perm))
        mine, = call(add_kernel, [half], landed)
        grads = call(
            functools.partial(merge_kernel, 3),
            [((rows, hidden_width), BF16)] * 3,
            [mine, exchange(mine, "dp", 1)],
            outside=True,
            scratch=[pltpu.VMEM((total, hidden_width), BF16)],
        )
    else:
        blocks = call(
            functools.partial(whole_parts_kernel, 3),
            [((3, rows, hidden_width), BF16)] * (fsdp // 2),
            [*kept, *received],
        )
        ready = blocks[0]
        landed = [exchange(blocks[mask], "fsdp", 2 * mask) for mask in range(1, fsdp // 2)]
        mine, = call(add_kernel, [(ready.shape, BF16)], [ready, *landed])
        grads = lax.psum(mine, "dp")

    back = []
    for mask in straight:
        total, = call(middle_kernel, [(part_shape, BF16)], [part[mask ^ 1], arrived[mask], ready])
        part[1], total = lax.optimization_barrier((part[1], total))
        back.append(exchange(total, "tensor", mask ^ 1))
    back.append(exchange(part[1], "tensor", 1))
    part[0], grads = lax.optimization_barrier((part[0], grads))
    mixed, grad_tokens = call(
        functools.partial(rows_sum_kernel, len(back)),
        [((width, own_count), BF16)] * 2,
        [part[0], *back],
        outside=True,
    )
    return mixed.T, grad_tokens.T, grads[0], grads[1], grads[2].T


def solution(mesh):
    token_spec = P(("dp", "fsdp", "tensor"), None)
    return jax.shard_map(
        per_device,
        mesh=mesh,
        in_specs=(token_spec, P("fsdp", "tensor"), P("fsdp", "tensor"), P("tensor", "fsdp"), token_spec),
        out_specs=(token_spec, token_spec, P("fsdp", "tensor"), P("fsdp", "tensor"), P("tensor", "fsdp")),
        check_vma=False,
    )
```

```python
import functools

import jax
import jax.numpy as jnp
from jax import lax
from jax.experimental import pallas as pl
from jax.experimental.pallas import tpu as pltpu
from jax.sharding import PartitionSpec as P

BF16, F32 = jnp.bfloat16, jnp.float32
SCOPED_BYTES = 16 * 1024 * 1024
SPARE = 16


def contract(left, right, left_dim, right_dim):
    return lax.dot_general(left, right, (((left_dim,), (right_dim,)), ((), ())), preferred_element_type=F32)


def exchange(array, axis, mask):
    return lax.ppermute(array, axis, [(i, i ^ mask) for i in range(lax.axis_size(axis))])


def call(body, outs, operands, inside=pltpu.VMEM, outside=False, scratch=()):
    whole = pl.BlockSpec(memory_space=pltpu.VMEM)
    kind = jax.ShapeDtypeStruct if outside else pltpu.VMEM
    return pl.pallas_call(
        body,
        out_shape=[kind(shape, dtype) for shape, dtype in outs],
        in_specs=[pl.BlockSpec(memory_space=inside)] * len(operands),
        out_specs=[whole] * len(outs),
        scratch_shapes=list(scratch),
        cost_estimate=pl.CostEstimate(flops=1, bytes_accessed=1, transcendentals=0),
        compiler_params=pltpu.CompilerParams(vmem_limit_bytes=SCOPED_BYTES),
    )(*[pltpu.with_memory_space_constraint(operand, inside) for operand in operands])


def stack_kernel(counts, twin, *refs):
    arrays, sems = refs[: sum(counts)], refs[-1]
    stacks = refs[len(arrays):len(arrays) + len(counts)]
    places = [stack.at[i] for stack, count in zip(stacks, counts) for i in range(count)]
    copies = [pltpu.make_async_copy(array, place, sems.at[i]) for i, (array, place) in enumerate(zip(arrays, places))]
    for copy in copies:
        copy.start()
    for copy in copies:
        copy.wait()
    if twin:
        refs[-2][:, :stacks[0].shape[1]] = stacks[0][...]


def stack(*groups, spare=0):
    arrays = [array for group in groups for array in group]
    outs = [((len(group), *group[0].shape), group[0].dtype) for group in groups]
    if spare:
        (count, rows, columns), dtype = outs[0]
        outs.append(((count, rows + spare, columns), dtype))
    return call(
        functools.partial(stack_kernel, [len(group) for group in groups], bool(spare)),
        outs,
        arrays,
        inside=pltpu.HBM,
        scratch=[pltpu.SemaphoreType.DMA((len(arrays),))],
    )


def join_kernel(*refs):
    runs, joined = refs[:-1], refs[-1]
    first = 0
    for run in runs:
        joined[first:first + run.shape[0]] = run[...]
        first += run.shape[0]


def assemble_kernel(masks, *refs):
    blocks, (whole, turned) = refs[: len(masks)], refs[len(masks):]
    index = lax.axis_index("fsdp")
    rows = blocks[0].shape[1]
    for mask, block in zip(masks, blocks):
        start = pl.multiple_of((index ^ mask) * rows, 16)
        whole[:, pl.ds(start, rows), :] = block[...]
    for i in range(whole.shape[0]):
        turned[i] = whole[i].T


def forward(turned, rows):
    gate_sum = contract(turned[0], rows, 1, 0)
    up_sum = contract(turned[1], rows, 1, 0)
    sig = 1.0 / (1.0 + jnp.exp(-gate_sum))
    swished = gate_sum * sig
    slopes = up_sum * sig * (1.0 + gate_sum * (1.0 - sig))
    return (swished * up_sum).astype(BF16), swished, slopes


def block_grads(turned, blocks):
    width = turned.shape[2]
    rows, columns = (jnp.concatenate([block[side, :width] for block in blocks], axis=1) for side in range(2))
    hidden, swished, slopes = forward(turned, rows)
    grad_hidden = contract(turned[2], columns, 1, 0)
    grad_gate = (grad_hidden * slopes).astype(BF16)
    grad_up = (grad_hidden * swished).astype(BF16)
    return rows, columns, hidden, grad_gate, grad_up


def token_parts(whole, hidden, grad_gate, grad_up, parts):
    out = contract(whole[2], hidden, 1, 0)
    back = contract(whole[0], grad_gate, 1, 0) + contract(whole[1], grad_up, 1, 0)
    width = out.shape[1] // len(parts)
    rows = out.shape[0]
    for i, part in enumerate(parts):
        part[0, :rows] = out[:, i * width:(i + 1) * width].astype(part.dtype)
        part[1, :rows] = back[:, i * width:(i + 1) * width].astype(part.dtype)
        if part.shape[1] > rows:
            part[:, rows:] = jnp.zeros((2, part.shape[1] - rows, width), part.dtype)


def weight_terms(rows, columns, hidden, grad_gate, grad_up):
    return ((rows, grad_gate), (rows, grad_up), (columns, hidden))


def group_kernel(count, first, whole, turned, *refs):
    blocks, refs = refs[:count], refs[count:]
    before, (after, *parts) = (None, refs) if first else (refs[0], refs[1:])
    rows, columns, hidden, grad_gate, grad_up = block_grads(turned, blocks)
    for i, (left, right) in enumerate(weight_terms(rows, columns, hidden, grad_gate, grad_up)):
        term = contract(left, right, 1, 1)
        after[i] = term if first else before[i] + term
    token_parts(whole, hidden, grad_gate, grad_up, parts)


def share_terms(pick, block, hidden, grad_gate, grad_up, before, outs):
    pairs, size = outs[0].shape[:2]
    for i, (side, right) in enumerate(((0, grad_gate), (0, grad_up), (1, hidden))):
        for pair in range(pairs):
            start = pl.multiple_of((2 * pair + pick) * size, 16)
            term = contract(block[side, pl.ds(start, size), :], right, 1, 1)
            outs[i][pair] = (before[i, pl.ds(start, size), :] + term).astype(outs[i].dtype)


def last_kernel(turned, block, before, hidden_out, gate_out, up_out, *outs):
    _, _, hidden, grad_gate, grad_up = block_grads(turned, [block])
    hidden_out[...], gate_out[...], up_out[...] = hidden, grad_gate, grad_up
    share_terms(1 - lax.axis_index("fsdp") % 2, block, hidden, grad_gate, grad_up, before, outs)


def kept_kernel(block, hidden, grad_gate, grad_up, before, *outs):
    own = lax.axis_index("fsdp") % 2
    share_terms(own, block, hidden[...], grad_gate[...], grad_up[...], before, outs)


def last_parts_kernel(whole, hidden, grad_gate, grad_up, part):
    token_parts(whole, hidden[...], grad_gate[...], grad_up[...], [part])


def pair_sums(count, refs):
    kept, received = refs[:count], refs[count:2 * count]
    return lambda i, pair: (kept[i][pair] + received[i][pair].astype(F32)).astype(BF16)


def whole_parts_kernel(count, *refs):
    sums, parts = pair_sums(count, refs), refs[2 * count:]
    index = lax.axis_index("fsdp") // 2
    for mask, part in enumerate(parts):
        for i in range(count):
            part[i] = sums(i, index ^ mask)


def split_parts_kernel(count, *refs):
    sums, parts, rows = pair_sums(count, refs), refs[2 * count:-1], refs[-1]
    index, own = lax.axis_index("fsdp") // 2, lax.axis_index("dp")
    size, length = rows.shape[0] // count, parts[0].shape[0]
    for mask in range(len(parts) // 2):
        for i in range(count):
            rows[i * size:(i + 1) * size] = sums(i, index ^ mask)
        for flip in range(2):
            start = pl.multiple_of((own ^ flip) * (rows.shape[0] - length), 16)
            parts[2 * mask + flip][...] = rows[pl.ds(start, length), :]


def add_kernel(*refs):
    total = refs[0][...].astype(F32)
    for ref in refs[1:-1]:
        total = total + ref[...].astype(F32)
    refs[-1][...] = total.astype(BF16)


def merge_kernel(count, mine, other, *refs):
    outs, rows = refs[:count], refs[count]
    first = lax.axis_index("dp") == 0
    length = mine.shape[0]
    rows[:length] = jnp.where(first, mine[...], other[...])
    rows[rows.shape[0] - length:] = jnp.where(first, other[...], mine[...])
    size = rows.shape[0] // count
    for i, out in enumerate(outs):
        out[...] = rows[i * size:(i + 1) * size]


def middle_kernel(part, received, *refs):
    total = refs[-1]
    total[...] = (part[...] + received[...].astype(F32)).astype(BF16)


def rows_sum_kernel(count, own, *refs):
    received, outs = refs[:count], refs[count:]
    for i, out in enumerate(outs):
        total = own[i]
        for ref in received:
            total = total + ref[i, :out.shape[0]].astype(F32)
        out[...] = total.astype(BF16)


def per_device(tokens, gate_weight, up_weight, down_weight, cotangent):
    tensor, fsdp, dp = (lax.axis_size(axis) for axis in ("tensor", "fsdp", "dp"))
    own_count, width = tokens.shape
    rows, hidden_width = gate_weight.shape

    block, weight = {}, {}
    own_weights = [gate_weight, up_weight, down_weight.T]
    block[0], near = stack([tokens.T, cotangent.T], spare=SPARE)
    weight[0], *runs = stack(own_weights, own_weights[:2], own_weights[2:])
    straight = list(range(3, tensor, 2))
    for mask in straight + [1]:
        block[mask] = exchange(near if mask == 1 else block[0], "tensor", mask)
    for mask in straight:
        block[mask], block[1] = lax.optimization_barrier((block[mask], block[1]))
        block[mask ^ 1] = exchange(block[mask], "tensor", 1)
    masks = list(range(fsdp))
    weight[1] = exchange(weight[0], "fsdp", 1)
    for mask in masks[2::2]:
        weight[mask], = call(
            join_kernel, [(weight[0].shape, BF16)], [exchange(run, "fsdp", mask) for run in runs]
        )
        weight[mask + 1] = exchange(weight[mask], "fsdp", 1)
    whole, turned = call(
        functools.partial(assemble_kernel, masks),
        [((3, width, hidden_width), BF16), ((3, hidden_width, width), BF16)],
        [weight[mask] for mask in masks],
    )

    part_shape = (2, width, own_count)
    sums_shape = ((3, width, hidden_width), F32)
    sums, part = [], {}
    forwarded = [mask ^ 1 for mask in straight]
    last = forwarded[-1]
    for group in [[0, 1]] + [[mask] for mask in straight + forwarded[:-1]]:
        kinds = {mask: (part_shape, BF16 if mask % 2 else F32) for mask in group}
        sums, *parts = call(
            functools.partial(group_kernel, len(group), 0 in group),
            [sums_shape] + [kinds[mask] for mask in group],
            [whole, turned] + [block[mask] for mask in group] + ([] if 0 in group else [sums]),
        )
        part.update(zip(group, parts))
    arrived = {}
    for mask in straight:
        part[mask], block[last] = lax.optimization_barrier((part[mask], block[last]))
        arrived[mask] = exchange(part[mask], "tensor", 1)
    half_shape = (fsdp // 2, rows, hidden_width)
    results = call(
        last_kernel,
        [((hidden_width, own_count), BF16)] * 3 + [(half_shape, BF16)] * 3,
        [turned, block[last], sums],
    )
    state, sent = list(results[:3]), results[3:]
    kept = call(kept_kernel, [(half_shape, F32)] * 3, [block[last], *state, sums])

    received = [exchange(array, "fsdp", 1) for array in sent]
    if dp == 2:
        total = 3 * rows
        length = (total // 2 + 15) // 16 * 16
        half = ((length, hidden_width), BF16)
        shares = call(
            functools.partial(split_parts_kernel, 3),
            [half] * fsdp,
            [*kept, *received],
            scratch=[pltpu.VMEM((total, hidden_width), BF16)],
        )
        ready = shares[0]
        landed = [ready]
        for i, share in list(enumerate(shares))[1:]:
            mask, flip = 2 * (i // 2), i % 2
            perm = [(d * fsdp + f, (d ^ flip) * fsdp + (f ^ mask)) for d in range(dp) for f in range(fsdp)]
            landed.append(lax.ppermute(share, ("dp", "fsdp"), perm))
        mine, = call(add_kernel, [half], landed)
        grads = call(
            functools.partial(merge_kernel, 3),
            [((rows, hidden_width), BF16)] * 3,
            [mine, exchange(mine, "dp", 1)],
            outside=True,
            scratch=[pltpu.VMEM((total, hidden_width), BF16)],
        )
    else:
        blocks = call(
            functools.partial(whole_parts_kernel, 3),
            [((3, rows, hidden_width), BF16)] * (fsdp // 2),
            [*kept, *received],
        )
        ready = blocks[0]
        landed = [exchange(blocks[mask], "fsdp", 2 * mask) for mask in range(1, fsdp // 2)]
        mine, = call(add_kernel, [(ready.shape, BF16)], [ready, *landed])
        grads = lax.psum(mine, "dp")

    back = []
    state[0], ready = lax.optimization_barrier((state[0], ready))
    part[last], = call(last_parts_kernel, [(part_shape, F32)], [whole, *state])
    for mask in straight:
        total, = call(middle_kernel, [(part_shape, BF16)], [part[mask ^ 1], arrived[mask], ready])
        part[1], total = lax.optimization_barrier((part[1], total))
        back.append(exchange(total, "tensor", mask ^ 1))
    back.append(exchange(part[1], "tensor", 1))
    part[0], grads = lax.optimization_barrier((part[0], grads))
    mixed, grad_tokens = call(
        functools.partial(rows_sum_kernel, len(back)),
        [((width, own_count), BF16)] * 2,
        [part[0], *back],
        outside=True,
    )
    return mixed.T, grad_tokens.T, grads[0], grads[1], grads[2].T


def solution(mesh):
    token_spec = P(("dp", "fsdp", "tensor"), None)
    return jax.shard_map(
        per_device,
        mesh=mesh,
        in_specs=(token_spec, P("fsdp", "tensor"), P("fsdp", "tensor"), P("tensor", "fsdp"), token_spec),
        out_specs=(token_spec, token_spec, P("fsdp", "tensor"), P("fsdp", "tensor"), P("tensor", "fsdp")),
        check_vma=False,
    )
```

```python
import functools

import jax
import jax.numpy as jnp
from jax import lax
from jax.experimental import pallas as pl
from jax.experimental.pallas import tpu as pltpu
from jax.sharding import PartitionSpec as P

BF16, F32 = jnp.bfloat16, jnp.float32
SCOPED_BYTES = 16 * 1024 * 1024
SPARE = 16


def contract(left, right, left_dim, right_dim):
    return lax.dot_general(left, right, (((left_dim,), (right_dim,)), ((), ())), preferred_element_type=F32)


def exchange(array, axis, mask):
    return lax.ppermute(array, axis, [(i, i ^ mask) for i in range(lax.axis_size(axis))])


def call(body, outs, operands, inside=pltpu.VMEM, outside=False, scratch=()):
    whole = pl.BlockSpec(memory_space=pltpu.VMEM)
    kind = jax.ShapeDtypeStruct if outside else pltpu.VMEM
    return pl.pallas_call(
        body,
        out_shape=[kind(shape, dtype) for shape, dtype in outs],
        in_specs=[pl.BlockSpec(memory_space=inside)] * len(operands),
        out_specs=[whole] * len(outs),
        scratch_shapes=list(scratch),
        cost_estimate=pl.CostEstimate(flops=1, bytes_accessed=1, transcendentals=0),
        compiler_params=pltpu.CompilerParams(vmem_limit_bytes=SCOPED_BYTES),
    )(*[pltpu.with_memory_space_constraint(operand, inside) for operand in operands])


def stack_kernel(counts, twin, *refs):
    arrays, sems = refs[: sum(counts)], refs[-1]
    stacks = refs[len(arrays):len(arrays) + len(counts)]
    places = [stack.at[i] for stack, count in zip(stacks, counts) for i in range(count)]
    copies = [pltpu.make_async_copy(array, place, sems.at[i]) for i, (array, place) in enumerate(zip(arrays, places))]
    for copy in copies:
        copy.start()
    for copy in copies:
        copy.wait()
    if twin:
        refs[-2][:, :stacks[0].shape[1]] = stacks[0][...]


def stack(*groups, spare=0):
    arrays = [array for group in groups for array in group]
    outs = [((len(group), *group[0].shape), group[0].dtype) for group in groups]
    if spare:
        (count, rows, columns), dtype = outs[0]
        outs.append(((count, rows + spare, columns), dtype))
    return call(
        functools.partial(stack_kernel, [len(group) for group in groups], bool(spare)),
        outs,
        arrays,
        inside=pltpu.HBM,
        scratch=[pltpu.SemaphoreType.DMA((len(arrays),))],
    )


def join_kernel(*refs):
    runs, joined = refs[:-1], refs[-1]
    first = 0
    for run in runs:
        joined[first:first + run.shape[0]] = run[...]
        first += run.shape[0]


def assemble_kernel(masks, *refs):
    blocks, (whole, turned) = refs[: len(masks)], refs[len(masks):]
    index = lax.axis_index("fsdp")
    rows = blocks[0].shape[1]
    for mask, block in zip(masks, blocks):
        start = pl.multiple_of((index ^ mask) * rows, 16)
        whole[:, pl.ds(start, rows), :] = block[...]
    for i in range(whole.shape[0]):
        turned[i] = whole[i].T


def forward(turned, rows):
    gate_sum = contract(turned[0], rows, 1, 0)
    up_sum = contract(turned[1], rows, 1, 0)
    sig = 1.0 / (1.0 + jnp.exp(-gate_sum))
    swished = gate_sum * sig
    slopes = up_sum * sig * (1.0 + gate_sum * (1.0 - sig))
    return (swished * up_sum).astype(BF16), swished, slopes


def block_grads(turned, blocks):
    width = turned.shape[2]
    rows, columns = (jnp.concatenate([block[side, :width] for block in blocks], axis=1) for side in range(2))
    hidden, swished, slopes = forward(turned, rows)
    grad_hidden = contract(turned[2], columns, 1, 0)
    grad_gate = (grad_hidden * slopes).astype(BF16)
    grad_up = (grad_hidden * swished).astype(BF16)
    return rows, columns, hidden, grad_gate, grad_up


def token_parts(whole, hidden, grad_gate, grad_up, parts):
    out = contract(whole[2], hidden, 1, 0)
    back = contract(whole[0], grad_gate, 1, 0) + contract(whole[1], grad_up, 1, 0)
    width = out.shape[1] // len(parts)
    rows = out.shape[0]
    for i, part in enumerate(parts):
        part[0, :rows] = out[:, i * width:(i + 1) * width].astype(part.dtype)
        part[1, :rows] = back[:, i * width:(i + 1) * width].astype(part.dtype)
        if part.shape[1] > rows:
            part[:, rows:] = jnp.zeros((2, part.shape[1] - rows, width), part.dtype)


def weight_terms(rows, columns, hidden, grad_gate, grad_up):
    return ((rows, grad_gate), (rows, grad_up), (columns, hidden))


def group_kernel(count, first, whole, turned, *refs):
    blocks, refs = refs[:count], refs[count:]
    before, (after, *parts) = (None, refs) if first else (refs[0], refs[1:])
    rows, columns, hidden, grad_gate, grad_up = block_grads(turned, blocks)
    for i, (left, right) in enumerate(weight_terms(rows, columns, hidden, grad_gate, grad_up)):
        term = contract(left, right, 1, 1)
        after[i] = term if first else before[i] + term
    token_parts(whole, hidden, grad_gate, grad_up, parts)


def share_terms(pick, block, hidden, grad_gate, grad_up, before, outs):
    pairs, size = outs[0].shape[:2]
    for i, (side, right) in enumerate(((0, grad_gate), (0, grad_up), (1, hidden))):
        for pair in range(pairs):
            start = pl.multiple_of((2 * pair + pick) * size, 16)
            term = contract(block[side, pl.ds(start, size), :], right, 1, 1)
            outs[i][pair] = (before[i, pl.ds(start, size), :] + term).astype(outs[i].dtype)


def last_kernel(turned, block, before, hidden_out, gate_out, up_out, *outs):
    _, _, hidden, grad_gate, grad_up = block_grads(turned, [block])
    hidden_out[...], gate_out[...], up_out[...] = hidden, grad_gate, grad_up
    share_terms(1 - lax.axis_index("fsdp") % 2, block, hidden, grad_gate, grad_up, before, outs)


def kept_kernel(whole, block, hidden, grad_gate, grad_up, before, *outs):
    values = hidden[...], grad_gate[...], grad_up[...]
    share_terms(lax.axis_index("fsdp") % 2, block, *values, before, outs[:-1])
    token_parts(whole, *values, outs[-1:])


def pair_sums(count, refs):
    kept, received = refs[:count], refs[count:2 * count]
    return lambda i, pair: (kept[i][pair] + received[i][pair].astype(F32)).astype(BF16)


def whole_parts_kernel(count, *refs):
    sums, parts = pair_sums(count, refs), refs[2 * count:]
    index = lax.axis_index("fsdp") // 2
    for mask, part in enumerate(parts):
        for i in range(count):
            part[i] = sums(i, index ^ mask)


def split_parts_kernel(count, *refs):
    sums, parts, rows = pair_sums(count, refs), refs[2 * count:-1], refs[-1]
    index, own = lax.axis_index("fsdp") // 2, lax.axis_index("dp")
    size, length = rows.shape[0] // count, parts[0].shape[0]
    for mask in range(len(parts) // 2):
        for i in range(count):
            rows[i * size:(i + 1) * size] = sums(i, index ^ mask)
        for flip in range(2):
            start = pl.multiple_of((own ^ flip) * (rows.shape[0] - length), 16)
            parts[2 * mask + flip][...] = rows[pl.ds(start, length), :]


def add_kernel(*refs):
    total = refs[0][...].astype(F32)
    for ref in refs[1:-1]:
        total = total + ref[...].astype(F32)
    refs[-1][...] = total.astype(BF16)


def merge_kernel(count, mine, other, *refs):
    outs, rows = refs[:count], refs[count]
    first = lax.axis_index("dp") == 0
    length = mine.shape[0]
    rows[:length] = jnp.where(first, mine[...], other[...])
    rows[rows.shape[0] - length:] = jnp.where(first, other[...], mine[...])
    size = rows.shape[0] // count
    for i, out in enumerate(outs):
        out[...] = rows[i * size:(i + 1) * size]


def middle_kernel(part, received, *refs):
    total = refs[-1]
    total[...] = (part[...] + received[...].astype(F32)).astype(BF16)


def rows_sum_kernel(count, own, *refs):
    received, outs = refs[:count], refs[count:]
    for i, out in enumerate(outs):
        total = own[i]
        for ref in received:
            total = total + ref[i, :out.shape[0]].astype(F32)
        out[...] = total.astype(BF16)


def per_device(tokens, gate_weight, up_weight, down_weight, cotangent):
    tensor, fsdp, dp = (lax.axis_size(axis) for axis in ("tensor", "fsdp", "dp"))
    own_count, width = tokens.shape
    rows, hidden_width = gate_weight.shape

    block, weight = {}, {}
    own_weights = [gate_weight, up_weight, down_weight.T]
    block[0], near = stack([tokens.T, cotangent.T], spare=SPARE)
    weight[0], *runs = stack(own_weights, own_weights[:2], own_weights[2:])
    straight = list(range(3, tensor, 2))
    for mask in straight + [1]:
        block[mask] = exchange(near if mask == 1 else block[0], "tensor", mask)
    for mask in straight:
        block[mask], block[1] = lax.optimization_barrier((block[mask], block[1]))
        block[mask ^ 1] = exchange(block[mask], "tensor", 1)
    masks = list(range(fsdp))
    for mask in masks[2::2]:
        weight[mask], = call(
            join_kernel, [(weight[0].shape, BF16)], [exchange(run, "fsdp", mask) for run in runs]
        )
        weight[0], weight[mask] = lax.optimization_barrier((weight[0], weight[mask]))
        weight[mask + 1] = exchange(weight[mask], "fsdp", 1)
    weight[1] = exchange(weight[0], "fsdp", 1)
    whole, turned = call(
        functools.partial(assemble_kernel, masks),
        [((3, width, hidden_width), BF16), ((3, hidden_width, width), BF16)],
        [weight[mask] for mask in masks],
    )

    part_shape = (2, width, own_count)
    sums_shape = ((3, width, hidden_width), F32)
    sums, part = [], {}
    forwarded = [mask ^ 1 for mask in straight]
    last = forwarded[-1]
    for group in [[0, 1]] + [[mask] for mask in straight + forwarded[:-1]]:
        kinds = {mask: (part_shape, BF16 if mask % 2 else F32) for mask in group}
        sums, *parts = call(
            functools.partial(group_kernel, len(group), 0 in group),
            [sums_shape] + [kinds[mask] for mask in group],
            [whole, turned] + [block[mask] for mask in group] + ([] if 0 in group else [sums]),
        )
        part.update(zip(group, parts))
    arrived = {}
    for mask in straight:
        part[mask], block[last] = lax.optimization_barrier((part[mask], block[last]))
        arrived[mask] = exchange(part[mask], "tensor", 1)
    half_shape = (fsdp // 2, rows, hidden_width)
    results = call(
        last_kernel,
        [((hidden_width, own_count), BF16)] * 3 + [(half_shape, BF16)] * 3,
        [turned, block[last], sums],
    )
    state, sent = results[:3], results[3:]
    *kept, part[last] = call(
        kept_kernel, [(half_shape, F32)] * 3 + [(part_shape, F32)], [whole, block[last], *state, sums]
    )

    received = [exchange(array, "fsdp", 1) for array in sent]
    if dp == 2:
        total = 3 * rows
        length = (total // 2 + 15) // 16 * 16
        half = ((length, hidden_width), BF16)
        shares = call(
            functools.partial(split_parts_kernel, 3),
            [half] * fsdp,
            [*kept, *received],
            scratch=[pltpu.VMEM((total, hidden_width), BF16)],
        )
        ready = shares[0]
        landed = [ready]
        for i, share in list(enumerate(shares))[1:]:
            mask, flip = 2 * (i // 2), i % 2
            perm = [(d * fsdp + f, (d ^ flip) * fsdp + (f ^ mask)) for d in range(dp) for f in range(fsdp)]
            landed.append(lax.ppermute(share, ("dp", "fsdp"), perm))
        mine, = call(add_kernel, [half], landed)
        grads = call(
            functools.partial(merge_kernel, 3),
            [((rows, hidden_width), BF16)] * 3,
            [mine, exchange(mine, "dp", 1)],
            outside=True,
            scratch=[pltpu.VMEM((total, hidden_width), BF16)],
        )
    else:
        blocks = call(
            functools.partial(whole_parts_kernel, 3),
            [((3, rows, hidden_width), BF16)] * (fsdp // 2),
            [*kept, *received],
        )
        ready = blocks[0]
        landed = [exchange(blocks[mask], "fsdp", 2 * mask) for mask in range(1, fsdp // 2)]
        mine, = call(add_kernel, [(ready.shape, BF16)], [ready, *landed])
        grads = lax.psum(mine, "dp")

    back = []
    for mask in straight:
        total, = call(middle_kernel, [(part_shape, BF16)], [part[mask ^ 1], arrived[mask], ready])
        part[1], total = lax.optimization_barrier((part[1], total))
        back.append(exchange(total, "tensor", mask ^ 1))
    back.append(exchange(part[1], "tensor", 1))
    part[0], grads = lax.optimization_barrier((part[0], grads))
    mixed, grad_tokens = call(
        functools.partial(rows_sum_kernel, len(back)),
        [((width, own_count), BF16)] * 2,
        [part[0], *back],
        outside=True,
    )
    return mixed.T, grad_tokens.T, grads[0], grads[1], grads[2].T


def solution(mesh):
    token_spec = P(("dp", "fsdp", "tensor"), None)
    return jax.shard_map(
        per_device,
        mesh=mesh,
        in_specs=(token_spec, P("fsdp", "tensor"), P("fsdp", "tensor"), P("tensor", "fsdp"), token_spec),
        out_specs=(token_spec, token_spec, P("fsdp", "tensor"), P("fsdp", "tensor"), P("tensor", "fsdp")),
        check_vma=False,
    )
```

```python
import functools

import jax
import jax.numpy as jnp
from jax import lax
from jax.experimental import pallas as pl
from jax.experimental.pallas import tpu as pltpu
from jax.sharding import PartitionSpec as P

BF16, F32 = jnp.bfloat16, jnp.float32
SCOPED_BYTES = 16 * 1024 * 1024
SPARE = 16


def contract(left, right, left_dim, right_dim):
    return lax.dot_general(left, right, (((left_dim,), (right_dim,)), ((), ())), preferred_element_type=F32)


def exchange(array, axis, mask):
    return lax.ppermute(array, axis, [(i, i ^ mask) for i in range(lax.axis_size(axis))])


def call(body, outs, operands, inside=pltpu.VMEM, outside=False, scratch=()):
    whole = pl.BlockSpec(memory_space=pltpu.VMEM)
    kind = jax.ShapeDtypeStruct if outside else pltpu.VMEM
    return pl.pallas_call(
        body,
        out_shape=[kind(shape, dtype) for shape, dtype in outs],
        in_specs=[pl.BlockSpec(memory_space=inside)] * len(operands),
        out_specs=[whole] * len(outs),
        scratch_shapes=list(scratch),
        cost_estimate=pl.CostEstimate(flops=1, bytes_accessed=1, transcendentals=0),
        compiler_params=pltpu.CompilerParams(vmem_limit_bytes=SCOPED_BYTES),
    )(*[pltpu.with_memory_space_constraint(operand, inside) for operand in operands])


def stack_kernel(counts, twin, *refs):
    arrays, sems = refs[: sum(counts)], refs[-1]
    stacks = refs[len(arrays):len(arrays) + len(counts)]
    places = [stack.at[i] for stack, count in zip(stacks, counts) for i in range(count)]
    copies = [pltpu.make_async_copy(array, place, sems.at[i]) for i, (array, place) in enumerate(zip(arrays, places))]
    for copy in copies:
        copy.start()
    for copy in copies:
        copy.wait()
    if twin:
        refs[-2][:, :stacks[0].shape[1]] = stacks[0][...]


def stack(*groups, spare=0):
    arrays = [array for group in groups for array in group]
    outs = [((len(group), *group[0].shape), group[0].dtype) for group in groups]
    if spare:
        (count, rows, columns), dtype = outs[0]
        outs.append(((count, rows + spare, columns), dtype))
    return call(
        functools.partial(stack_kernel, [len(group) for group in groups], bool(spare)),
        outs,
        arrays,
        inside=pltpu.HBM,
        scratch=[pltpu.SemaphoreType.DMA((len(arrays),))],
    )


def join_kernel(*refs):
    runs, joined = refs[:-1], refs[-1]
    first = 0
    for run in runs:
        joined[first:first + run.shape[0]] = run[...]
        first += run.shape[0]


def assemble_kernel(masks, *refs):
    blocks, (whole, turned) = refs[: len(masks)], refs[len(masks):]
    index = lax.axis_index("fsdp")
    rows = blocks[0].shape[1]
    for mask, block in zip(masks, blocks):
        start = pl.multiple_of((index ^ mask) * rows, 16)
        whole[:, pl.ds(start, rows), :] = block[...]
    for i in range(whole.shape[0]):
        turned[i] = whole[i].T


def forward(turned, rows):
    gate_sum = contract(turned[0], rows, 1, 0)
    up_sum = contract(turned[1], rows, 1, 0)
    sig = 1.0 / (1.0 + jnp.exp(-gate_sum))
    swished = gate_sum * sig
    slopes = up_sum * sig * (1.0 + gate_sum * (1.0 - sig))
    return (swished * up_sum).astype(BF16), swished, slopes


def block_grads(turned, blocks):
    width = turned.shape[2]
    rows, columns = (jnp.concatenate([block[side, :width] for block in blocks], axis=1) for side in range(2))
    hidden, swished, slopes = forward(turned, rows)
    grad_hidden = contract(turned[2], columns, 1, 0)
    grad_gate = (grad_hidden * slopes).astype(BF16)
    grad_up = (grad_hidden * swished).astype(BF16)
    return rows, columns, hidden, grad_gate, grad_up


def token_parts(whole, hidden, grad_gate, grad_up, parts):
    out = contract(whole[2], hidden, 1, 0)
    back = contract(whole[0], grad_gate, 1, 0) + contract(whole[1], grad_up, 1, 0)
    width = out.shape[1] // len(parts)
    rows = out.shape[0]
    for i, part in enumerate(parts):
        part[0, :rows] = out[:, i * width:(i + 1) * width].astype(part.dtype)
        part[1, :rows] = back[:, i * width:(i + 1) * width].astype(part.dtype)
        if part.shape[1] > rows:
            part[:, rows:] = jnp.zeros((2, part.shape[1] - rows, width), part.dtype)


def weight_terms(rows, columns, hidden, grad_gate, grad_up):
    return ((rows, grad_gate), (rows, grad_up), (columns, hidden))


def group_kernel(count, first, whole, turned, *refs):
    blocks, refs = refs[:count], refs[count:]
    before, (after, *parts) = (None, refs) if first else (refs[0], refs[1:])
    rows, columns, hidden, grad_gate, grad_up = block_grads(turned, blocks)
    for i, (left, right) in enumerate(weight_terms(rows, columns, hidden, grad_gate, grad_up)):
        term = contract(left, right, 1, 1)
        after[i] = term if first else before[i] + term
    token_parts(whole, hidden, grad_gate, grad_up, parts)


def share_terms(pick, block, hidden, grad_gate, grad_up, before, outs):
    pairs, size = outs[0].shape[:2]
    for i, (side, right) in enumerate(((0, grad_gate), (0, grad_up), (1, hidden))):
        for pair in range(pairs):
            start = pl.multiple_of((2 * pair + pick) * size, 16)
            term = contract(block[side, pl.ds(start, size), :], right, 1, 1)
            outs[i][pair] = (before[i, pl.ds(start, size), :] + term).astype(outs[i].dtype)


def last_kernel(turned, block, before, hidden_out, gate_out, up_out, *outs):
    _, _, hidden, grad_gate, grad_up = block_grads(turned, [block])
    hidden_out[...], gate_out[...], up_out[...] = hidden, grad_gate, grad_up
    share_terms(1 - lax.axis_index("fsdp") % 2, block, hidden, grad_gate, grad_up, before, outs)


def kept_kernel(whole, block, hidden, grad_gate, grad_up, before, *outs):
    values = hidden[...], grad_gate[...], grad_up[...]
    share_terms(lax.axis_index("fsdp") % 2, block, *values, before, outs[:-1])
    token_parts(whole, *values, outs[-1:])


def pair_sums(count, refs):
    kept, received = refs[:count], refs[count:2 * count]
    return lambda i, pair: (kept[i][pair] + received[i][pair].astype(F32)).astype(BF16)


def whole_parts_kernel(count, *refs):
    sums, parts = pair_sums(count, refs), refs[2 * count:]
    index = lax.axis_index("fsdp") // 2
    for mask, part in enumerate(parts):
        for i in range(count):
            part[i] = sums(i, index ^ mask)


def split_parts_kernel(count, *refs):
    sums, parts, rows = pair_sums(count, refs), refs[2 * count:-1], refs[-1]
    index, own = lax.axis_index("fsdp") // 2, lax.axis_index("dp")
    size, length = rows.shape[0] // count, parts[0].shape[0]
    for mask in range(len(parts) // 2):
        for i in range(count):
            rows[i * size:(i + 1) * size] = sums(i, index ^ mask)
        for flip in range(2):
            start = pl.multiple_of((own ^ flip) * (rows.shape[0] - length), 16)
            parts[2 * mask + flip][...] = rows[pl.ds(start, length), :]


def add_kernel(*refs):
    total = refs[0][...].astype(F32)
    for ref in refs[1:-1]:
        total = total + ref[...].astype(F32)
    refs[-1][...] = total.astype(BF16)


def merge_kernel(count, mine, other, *refs):
    outs, rows = refs[:count], refs[count]
    first = lax.axis_index("dp") == 0
    length = mine.shape[0]
    rows[:length] = jnp.where(first, mine[...], other[...])
    rows[rows.shape[0] - length:] = jnp.where(first, other[...], mine[...])
    size = rows.shape[0] // count
    for i, out in enumerate(outs):
        out[...] = rows[i * size:(i + 1) * size]


def middle_kernel(part, received, *refs):
    total = refs[-1]
    total[...] = (part[...] + received[...].astype(F32)).astype(BF16)


def rows_sum_kernel(count, own, *refs):
    received, outs = refs[:count], refs[count:]
    for i, out in enumerate(outs):
        total = own[i]
        for ref in received:
            total = total + ref[i, :out.shape[0]].astype(F32)
        out[...] = total.astype(BF16)


def per_device(tokens, gate_weight, up_weight, down_weight, cotangent):
    tensor, fsdp, dp = (lax.axis_size(axis) for axis in ("tensor", "fsdp", "dp"))
    own_count, width = tokens.shape
    rows, hidden_width = gate_weight.shape

    block, weight = {}, {}
    own_weights = [gate_weight, up_weight, down_weight.T]
    block[0], near = stack([tokens.T, cotangent.T], spare=SPARE)
    weight[0], *runs = stack(own_weights, own_weights[:2], own_weights[2:])
    straight = list(range(3, tensor, 2))
    for mask in straight + [1]:
        block[mask] = exchange(near if mask == 1 else block[0], "tensor", mask)
    for mask in straight:
        block[mask], block[1] = lax.optimization_barrier((block[mask], block[1]))
        block[mask ^ 1] = exchange(block[mask], "tensor", 1)
    masks = list(range(fsdp))
    for mask in masks[2::2]:
        weight[mask], = call(
            join_kernel, [(weight[0].shape, BF16)], [exchange(run, "fsdp", mask) for run in runs]
        )
        weight[0], weight[mask] = lax.optimization_barrier((weight[0], weight[mask]))
        weight[mask + 1] = exchange(weight[mask], "fsdp", 1)
    weight[1] = exchange(weight[0], "fsdp", 1)
    whole, turned = call(
        functools.partial(assemble_kernel, masks),
        [((3, width, hidden_width), BF16), ((3, hidden_width, width), BF16)],
        [weight[mask] for mask in masks],
    )

    part_shape = (2, width, own_count)
    sums_shape = ((3, width, hidden_width), F32)
    sums, part = [], {}
    forwarded = [mask ^ 1 for mask in straight]
    last = forwarded[-1]
    for group in [[0, 1]] + [[mask] for mask in straight + forwarded[:-1]]:
        kinds = {mask: (part_shape, BF16 if mask % 2 else F32) for mask in group}
        sums, *parts = call(
            functools.partial(group_kernel, len(group), 0 in group),
            [sums_shape] + [kinds[mask] for mask in group],
            [whole, turned] + [block[mask] for mask in group] + ([] if 0 in group else [sums]),
        )
        part.update(zip(group, parts))
    arrived = {}
    for mask in straight:
        part[mask], block[last] = lax.optimization_barrier((part[mask], block[last]))
        arrived[mask] = exchange(part[mask], "tensor", 1)
    half_shape = (fsdp // 2, rows, hidden_width)
    results = call(
        last_kernel,
        [((hidden_width, own_count), BF16)] * 3 + [(half_shape, BF16)] * 3,
        [turned, block[last], sums],
    )
    state, sent = results[:3], results[3:]
    *kept, part[last] = call(
        kept_kernel, [(half_shape, F32)] * 3 + [(part_shape, F32)], [whole, block[last], *state, sums]
    )

    received = [exchange(array, "fsdp", 1) for array in sent]
    if dp == 2:
        total = 3 * rows
        length = (total // 2 + 15) // 16 * 16
        half = ((length, hidden_width), BF16)
        shares = call(
            functools.partial(split_parts_kernel, 3),
            [half] * fsdp,
            [*kept, *received],
            scratch=[pltpu.VMEM((total, hidden_width), BF16)],
        )
        ready = shares[0]
        landed = [ready]
        for i, share in reversed(list(enumerate(shares))[1:]):
            mask, flip = 2 * (i // 2), i % 2
            perm = [(d * fsdp + f, (d ^ flip) * fsdp + (f ^ mask)) for d in range(dp) for f in range(fsdp)]
            landed.append(lax.ppermute(share, ("dp", "fsdp"), perm))
        mine, = call(add_kernel, [half], landed)
        grads = call(
            functools.partial(merge_kernel, 3),
            [((rows, hidden_width), BF16)] * 3,
            [mine, exchange(mine, "dp", 1)],
            outside=True,
            scratch=[pltpu.VMEM((total, hidden_width), BF16)],
        )
    else:
        blocks = call(
            functools.partial(whole_parts_kernel, 3),
            [((3, rows, hidden_width), BF16)] * (fsdp // 2),
            [*kept, *received],
        )
        ready = blocks[0]
        landed = [exchange(blocks[mask], "fsdp", 2 * mask) for mask in range(1, fsdp // 2)]
        mine, = call(add_kernel, [(ready.shape, BF16)], [ready, *landed])
        grads = lax.psum(mine, "dp")

    back = []
    for mask in straight:
        total, = call(middle_kernel, [(part_shape, BF16)], [part[mask ^ 1], arrived[mask], ready])
        part[1], total = lax.optimization_barrier((part[1], total))
        back.append(exchange(total, "tensor", mask ^ 1))
    back.append(exchange(part[1], "tensor", 1))
    part[0], grads = lax.optimization_barrier((part[0], grads))
    mixed, grad_tokens = call(
        functools.partial(rows_sum_kernel, len(back)),
        [((width, own_count), BF16)] * 2,
        [part[0], *back],
        outside=True,
    )
    return mixed.T, grad_tokens.T, grads[0], grads[1], grads[2].T


def solution(mesh):
    token_spec = P(("dp", "fsdp", "tensor"), None)
    return jax.shard_map(
        per_device,
        mesh=mesh,
        in_specs=(token_spec, P("fsdp", "tensor"), P("fsdp", "tensor"), P("tensor", "fsdp"), token_spec),
        out_specs=(token_spec, token_spec, P("fsdp", "tensor"), P("fsdp", "tensor"), P("tensor", "fsdp")),
        check_vma=False,
    )
```
